128 devices in a mesh: ctx: 8 (over z, x_lo), kvh: 2 (over x_hi), exp: 8 (over y, core).
Axes of the slice: x: 4 (x_hi: 2, x_lo: 2; x = x_hi * 2 + x_lo), y: 4, z: 4, core: 2. Of those that a mesh axis runs over, the one named last changes fastest.
Arguments:
- queries: bfloat16 [32, 4, 8, 128], P('exp', 'kvh'), may hold values from -72 to 72
- key_cache: bfloat16 [32, 8192, 4, 128], P('exp', 'ctx', 'kvh'), may hold values from -6 to 6
- value_cache: bfloat16 [32, 8192, 4, 128], P('exp', 'ctx', 'kvh'), may hold values from -6 to 6
- centroid_keys: bfloat16 [32, 512, 4, 128], P('exp', 'ctx', 'kvh'), may hold values from -3 to 3
- centroid_values: bfloat16 [32, 512, 4, 128], P('exp', 'ctx', 'kvh'), may hold values from -6 to 6
- selected: int32 [32, 4, 16], P('exp', 'kvh', 'ctx'), may hold values from 0 to 511, as said below
- new_key: bfloat16 [32, 4, 128], P('exp', 'kvh'), may hold values from -6 to 6
- new_value: bfloat16 [32, 4, 128], P('exp', 'kvh'), may hold values from -6 to 6
- out_weight: bfloat16 [4, 8, 128, 4096], P('kvh', 'ctx'), may hold values from -0.5 to 0.5
- residual: bfloat16 [32, 4096], P('exp'), may hold values from -6 to 6
- norm_gain: float32 [4096], replicated, may hold values from 0.5 to 1.5
- expert_ids: int32 [32, 8], P('exp'), may hold values from 0 to 63, all different within a row; in each aligned block of 4 rows (0 to 3, 4 to 7, ...) at most 2 rows name the same one
- gate_weights: float32 [32, 8], P('exp'), may hold values from 0.05 to 0.5
- w_gate_up: bfloat16 [64, 4096, 2, 1536], P(('ctx', 'exp'), None, None, 'kvh'), may hold values from -0.09375 to 0.09375
- w_down: bfloat16 [64, 1536, 4096], P(('ctx', 'exp'), 'kvh'), may hold values from -0.15625 to 0.15625
Outputs:
- layer_out: bfloat16 [32, 4096], P('exp', ('ctx', 'kvh'))
The draws below stay inside these ranges and needn't reach their ends.
Inputs may be any that keep to these rules, and one draw needn't show every extreme that they name: `selected`: entries k * 2 to (k + 1) * 2 - 1 of each list are different clusters held by context shard k, that is numbers from k * 64 to (k + 1) * 64 - 1. `expert_ids`: in the 4 rows of one index of exp no expert is named by more than 2 rows, a bound that some block reaches of them.
All inputs are finite; a program needn't handle non-finite values.
Results may differ from the reference program's by a relative error of at most 0.02.
Values may be sent and summed in bfloat16 or wider, within the bound.
No kernel may reach another device: no remote copies, remote signals or barrier semaphores. Data moves between devices by JAX's collectives and lax.ppermute only.
A program may use at most 128 MiB of HBM per device.

```python
import math
import jax
import jax.numpy as jnp
import numpy as np
from jax import lax

D = 4096
HD = 128
KVH = 4
QPG = 8
HID = 1536
TOP = 8
CSIZE = 16
SEL_DEV = 2
SEQ_DEV = 4
ROWS = 32
CTXLEN = 8192
CL_DEV = 64
CLUS = 512
NSEL = 16
EXPERTS = 64
CAP = 2
N_EXP = 8


def centroid_base(key):
    return jax.random.truncated_normal(jax.random.fold_in(key, 100), -3.0, 3.0, (ROWS, CLUS, KVH, HD), jnp.float32)


def draw_centroid_keys(key, part):
    base = centroid_base(key)
    return base.astype(jnp.bfloat16)


def draw_queries(key, part):
    key = jax.random.fold_in(key, 2)
    return jax.random.truncated_normal(key, -3.0, 3.0, (ROWS, KVH, QPG, HD), jnp.float32).astype(jnp.bfloat16)


def draw_selected(key, part):
    key = jax.random.fold_in(key, 3)
    shards = CLUS // CL_DEV
    random_keys = jax.random.randint(key, (ROWS, KVH, shards, CL_DEV), 0, 1 << 20)
    scores = random_keys * CL_DEV + jnp.arange(CL_DEV, dtype=jnp.int32)
    ranked = jnp.argsort(scores, axis=-1)[..., :SEL_DEV].astype(jnp.int32)
    offsets = (jnp.arange(shards, dtype=jnp.int32) * CL_DEV)[None, None, :, None]
    return (ranked + offsets).reshape(ROWS, KVH, shards * SEL_DEV)


def block_levels(stream_key, shape, cuts, least, high):
    loudness = 1.0
    for dim, shards_of in cuts:
        heights = jax.random.uniform(jax.random.fold_in(jax.random.fold_in(stream_key, 6), dim), (shards_of,), jnp.float32, least / len(cuts), high / len(cuts))
        loudness = loudness * jnp.repeat(jnp.exp(heights), shape[dim] // shards_of).reshape((-1,) + (1,) * (len(shape) - 1 - dim))
    return loudness


def assign_block(own_key, own, number, rows, count, top, bound, lean):
    ranking = jax.random.permutation(own_key, count)
    heavy_load, usual = shares(count, rows * top, bound, lean, True), shares(count, rows * top, bound, lean, False)
    places = jnp.arange(count)

    def named(sizes, turn):
        used = int((sizes > 0).sum())
        fixed = max(1, used // 4)
        shifted = fixed + (places - fixed + turn * (used - fixed)) % max(1, count - fixed)
        return jnp.zeros((count,), jnp.int32).at[ranking[jnp.where(places < fixed, places, shifted)]].set(jnp.asarray(sizes, jnp.int32))

    sizes = jnp.where(number % 4 == 0, named(heavy_load, number // 4), named(usual, number - number // 4 - 1))
    mixed = jax.random.permutation(jax.random.fold_in(own, 3), count)
    donor, receiver = mixed[0:count // 2 * 2:2], mixed[1:count // 2 * 2:2]
    room = jnp.minimum(sizes[donor] - 1, bound - sizes[receiver]) // 2
    room = jnp.where((donor == ranking[0]) | (receiver == ranking[0]) | (sizes[receiver] == 0), 0, jnp.maximum(room, 0))
    shifted = jax.random.randint(jax.random.fold_in(own, 4), (count // 2,), 0, 1 << 20) % (room + 1)
    sizes = sizes.at[donor].add(-shifted).at[receiver].add(shifted)
    items = jnp.searchsorted(jnp.cumsum(sizes), jnp.arange(rows * top), side="right").astype(jnp.int32)
    listing = items.reshape(top, rows).T
    listing = listing[jax.random.permutation(jax.random.fold_in(own, 1), rows)]
    turn = jax.random.randint(jax.random.fold_in(own, 2), (rows, 1), 0, top)
    return jnp.take_along_axis(listing, (jnp.arange(top)[None, :] + turn) % top, axis=1)


def shares(number_of, total, bound, slope, full):
    weights = [(1 << 20) // math.isqrt(rank ** slope) + 1 for rank in range(1, number_of + 1)]
    largest = bound if full else min(bound, max(-(-total // number_of), total * weights[0] // sum(weights)))
    least = 1 if total - largest >= number_of - 1 else 0
    counts, spare = [largest] + [least] * (number_of - 1), total - largest - least * (number_of - 1)
    while spare > 0:
        candidates = [i for i in range(1, number_of) if counts[i] < largest] or [i for i in range(1, number_of) if counts[i] < bound]
        mass, remaining = sum([weights[i] for i in candidates]), spare
        for i in candidates:
            addition = min(bound - counts[i], max(1, remaining * weights[i] // mass), spare)
            counts[i] = counts[i] + addition
            spare = spare - addition
    return np.array(counts)


def noise(key, dims, spread, reach, pieces=(), kind=jnp.bfloat16):
    level = block_levels(key, dims, pieces, -0.22, 0.18) if pieces else 1.0
    entries = jax.random.normal(key, dims, jnp.float32) * spread * level
    return jnp.minimum(jnp.maximum(entries, -reach), reach).astype(kind)


def setup_inputs(seed: int = 0) -> dict:
    splits = jax.random.split(jax.random.key(seed), 16)
    queries = draw_queries(jax.random.fold_in(splits[15], 71), 0)
    key_cache = noise(splits[1], (ROWS, CTXLEN, KVH, HD), 1.0, 6.0, ((0, 8), (1, 8), (2, 2)))
    value_cache = noise(splits[2], (ROWS, CTXLEN, KVH, HD), 1.0, 6.0, ((0, 8), (1, 8), (2, 2)))
    centroid_keys = draw_centroid_keys(jax.random.fold_in(splits[15], 71), 0)
    centroid_values = noise(splits[4], (ROWS, CLUS, KVH, HD), 1.0, 6.0, ((0, 8), (1, 8), (2, 2)))
    selected = draw_selected(jax.random.fold_in(splits[15], 71), 0)
    new_key = noise(splits[6], (ROWS, KVH, HD), 1.0, 6.0, ((0, 8), (1, 2)))
    new_value = noise(splits[7], (ROWS, KVH, HD), 1.0, 6.0, ((0, 8), (1, 2)))
    out_weight = noise(splits[8], (KVH, QPG, HD, D), HD ** -0.5, 0.5, ((0, 2), (1, 8)))
    residual = noise(splits[9], (ROWS, D), 1.0, 6.0, ((0, 8),))
    norm_gain = jnp.clip(1.0 + 0.1 * jax.random.normal(splits[10], (D,), jnp.float32), 0.5, 1.5)
    expert_ids_keys = jax.random.split(jax.random.fold_in(splits[11], 1), ROWS // SEQ_DEV)
    expert_ids_turns = jax.random.permutation(jax.random.fold_in(splits[11], 3), ROWS // SEQ_DEV)
    expert_ids = jax.vmap(lambda own, number: assign_block(jax.random.fold_in(splits[11], 2), own, number, SEQ_DEV, EXPERTS, TOP, CAP, 2))(expert_ids_keys, expert_ids_turns).reshape((ROWS, TOP))
    gate_weights = jnp.clip(jnp.exp(math.log(0.5) - 2.3025851 * jax.random.uniform(splits[12], (ROWS, TOP), jnp.float32) ** block_levels(splits[12], (ROWS, TOP), ((0, 8),), -0.2, 0.2)), 0.05, 0.5)
    w_gate_up = noise(splits[13], (EXPERTS, D, 2, HID), D ** -0.5, 0.09375, ((0, 64), (3, 2)))
    w_down = noise(splits[14], (EXPERTS, HID, D), HID ** -0.5, 0.15625, ((0, 64), (1, 2)))
    return dict(queries=queries, key_cache=key_cache, value_cache=value_cache, centroid_keys=centroid_keys, centroid_values=centroid_values, selected=selected, new_key=new_key, new_value=new_value, out_weight=out_weight, residual=residual, norm_gain=norm_gain, expert_ids=expert_ids, gate_weights=gate_weights, w_gate_up=w_gate_up, w_down=w_down)


def reference(queries, key_cache, value_cache, centroid_keys, centroid_values, selected, new_key, new_value, out_weight, residual, norm_gain, expert_ids, gate_weights, w_gate_up, w_down):
    score_scale = 1.0 / math.sqrt(HD)
    query_f32 = queries.astype(jnp.float32)
    block_index = jnp.transpose(selected, (0, 2, 1))[:, :, None, :, None]
    key_blocks = key_cache.reshape(ROWS, CLUS, CSIZE, KVH, HD)
    value_blocks = value_cache.reshape(ROWS, CLUS, CSIZE, KVH, HD)
    picked_keys = jnp.take_along_axis(key_blocks, block_index, axis=1).reshape(ROWS, NSEL * CSIZE, KVH, HD)
    picked_values = jnp.take_along_axis(value_blocks, block_index, axis=1).reshape(ROWS, NSEL * CSIZE, KVH, HD)
    all_keys = jnp.concatenate([centroid_keys, picked_keys], 1).astype(jnp.float32)
    all_values = jnp.concatenate([centroid_values, picked_values], 1).astype(jnp.float32)
    scores = jnp.einsum('rgqd,rjgd->rgqj', query_f32, all_keys) * score_scale
    own_score = jnp.einsum('rgqd,rgd->rgq', query_f32, new_key.astype(jnp.float32)) * score_scale
    scores = jnp.concatenate([scores, own_score[..., None]], -1)
    probs = jax.nn.softmax(scores, axis=-1)
    attended = jnp.einsum('rgqj,rjgd->rgqd', probs[..., :-1], all_values)
    attended = attended + probs[..., -1:] * new_value.astype(jnp.float32)[:, :, None, :]
    attended = attended.astype(jnp.bfloat16)
    projected = jnp.dot(attended.reshape(ROWS, KVH * QPG * HD), out_weight.reshape(KVH * QPG * HD, D), preferred_element_type=jnp.float32)
    hidden1 = residual.astype(jnp.float32) + projected
    mean_square = lax.optimization_barrier(jnp.mean(hidden1 * hidden1, axis=-1, keepdims=True))
    normed = (hidden1 * lax.rsqrt(mean_square + 1e-06) * norm_gain.astype(jnp.float32)).astype(jnp.bfloat16)
    slots_most = N_EXP * CAP

    def one_expert(expert_mix, expert):
        matches = expert_ids == expert
        chosen = jnp.any(matches, axis=1)
        gate_row = lax.optimization_barrier(jnp.sum(jnp.where(matches, gate_weights, jnp.zeros_like(gate_weights)), axis=1))
        row_picks = jnp.nonzero(chosen, size=slots_most, fill_value=0)[0]
        filled = jnp.arange(slots_most) < jnp.sum(chosen.astype(jnp.int32))
        picked_rows = normed[row_picks]
        gate_up_out = jnp.dot(picked_rows, w_gate_up[expert].reshape(D, 2 * HID), preferred_element_type=jnp.float32)
        activated = (jax.nn.silu(gate_up_out[:, :HID]) * gate_up_out[:, HID:]).astype(jnp.bfloat16)
        outputs = jnp.dot(activated, w_down[expert], preferred_element_type=jnp.float32)
        row_gate = jnp.where(filled, gate_row[row_picks], jnp.zeros_like(gate_row[row_picks]))
        return (expert_mix.at[row_picks].add(outputs * row_gate[:, None]), None)
    expert_mix = lax.scan(one_expert, jnp.zeros((ROWS, D), jnp.float32), jnp.arange(EXPERTS, dtype=jnp.int32))[0]
    return (hidden1 + expert_mix).astype(jnp.bfloat16)
```

```python
import functools
import math

import jax
import jax.numpy as jnp
from jax import lax
from jax.experimental import pallas as pl
from jax.experimental.pallas import tpu as pltpu
from jax.sharding import PartitionSpec as P

VMEM_SPEC = pl.BlockSpec(memory_space=pltpu.VMEM)
SMEM_SPEC = pl.BlockSpec(memory_space=pltpu.SMEM)
ANY_SPEC = pl.BlockSpec(memory_space=pl.ANY)
MASKED = -1e30


def attention_kernel(
    selected,
    queries,
    new_key,
    new_value,
    centroid_keys,
    centroid_values,
    key_cache,
    value_cache,
    out,
    keys,
    values,
    picked_sem,
    centroid_sem,
):
    seq_count, heads_kv, query_count, head_dim = queries.shape
    clusters = centroid_keys.shape[1]
    sel_count = selected.shape[2]
    block_len = key_cache.shape[1] // clusters
    ctx_pos = lax.axis_index("ctx")
    copies = []
    for which, (source, held) in enumerate(((centroid_keys, keys), (centroid_values, values))):
        copies.append(
            pltpu.make_async_copy(source, held.at[:, pl.ds(0, clusters)], centroid_sem.at[which])
        )
    for s in range(seq_count):
        for g in range(heads_kv):
            for j in range(sel_count):
                block = selected[s, g, j] - ctx_pos * clusters
                place = clusters + (g * sel_count + j) * block_len
                for which, (source, held) in enumerate(((key_cache, keys), (value_cache, values))):
                    copies.append(
                        pltpu.make_async_copy(
                            source.at[s, pl.ds(block * block_len, block_len)],
                            held.at[s, pl.ds(place, block_len)],
                            picked_sem.at[which, s, g * sel_count + j],
                        )
                    )
    for copy in copies:
        copy.start()
    for copy in copies:
        copy.wait()
    positions = keys.shape[1]
    rows = positions * heads_kv
    flat_keys = keys.reshape(seq_count, rows, head_dim)
    flat_values = values.reshape(seq_count, rows, head_dim)
    shape = (heads_kv * query_count, rows)
    head_of_query = lax.broadcasted_iota(jnp.int32, shape, 0) // query_count
    column = lax.broadcasted_iota(jnp.int32, shape, 1)
    head_of_row = column % heads_kv
    position = column // heads_kv
    head_of_block = (position - clusters) // (sel_count * block_len)
    valid = (head_of_row == head_of_query) & (
        (position < clusters) | (head_of_block == head_of_query)
    )
    score_scale = 1.0 / math.sqrt(head_dim)
    for s in range(seq_count):
        query = queries[s].reshape(heads_kv * query_count, head_dim)
        scores = lax.dot_general(
            query, flat_keys[s], (((1,), (1,)), ((), ())), preferred_element_type=jnp.float32
        )
        scores = jnp.where(valid, scores * score_scale, MASKED)
        own = jnp.sum(
            queries[s].astype(jnp.float32) * new_key[s].astype(jnp.float32)[:, None, :],
            axis=-1,
            keepdims=True,
        ).reshape(heads_kv * query_count, 1)
        own = jnp.where(ctx_pos == 0, own * score_scale, MASKED)
        peak = jnp.maximum(jnp.max(scores, axis=-1, keepdims=True), own)
        probs = jnp.exp(scores - peak)
        own_prob = jnp.exp(own - peak)
        total = jnp.sum(probs, axis=-1, keepdims=True) + own_prob
        weighted = jnp.dot(
            probs.astype(jnp.bfloat16), flat_values[s], preferred_element_type=jnp.float32
        )
        own_value = jnp.broadcast_to(
            new_value[s].astype(jnp.float32)[:, None, :], (heads_kv, query_count, head_dim)
        ).reshape(heads_kv * query_count, head_dim)
        weighted = weighted + own_prob * own_value
        lane = lax.broadcasted_iota(jnp.int32, weighted.shape, 1)
        stats = jnp.where(lane < head_dim // 2, peak, total)
        for g in range(heads_kv):
            part = slice(g * query_count, (g + 1) * query_count)
            out[:, g * seq_count + s, :] = weighted[part]
            out[:, (heads_kv + g) * seq_count + s, :] = stats[part]


def attention(queries, key_cache, value_cache, centroid_keys, centroid_values, selected, new_key, new_value):
    seq_count, heads_kv, query_count, head_dim = queries.shape
    clusters = centroid_keys.shape[1]
    sel_count = selected.shape[2]
    block_len = key_cache.shape[1] // clusters
    held = pltpu.VMEM(
        (seq_count, clusters + heads_kv * sel_count * block_len, heads_kv, head_dim), jnp.bfloat16
    )
    return pl.pallas_call(
        attention_kernel,
        out_shape=jax.ShapeDtypeStruct((query_count, 2 * heads_kv * seq_count, head_dim), jnp.float32),
        in_specs=[SMEM_SPEC, VMEM_SPEC, VMEM_SPEC, VMEM_SPEC] + [ANY_SPEC] * 4,
        out_specs=VMEM_SPEC,
        scratch_shapes=[
            held,
            held,
            pltpu.SemaphoreType.DMA((2, seq_count, heads_kv * sel_count)),
            pltpu.SemaphoreType.DMA((2,)),
        ],
        compiler_params=pltpu.CompilerParams(vmem_limit_bytes=8 << 20),
    )(selected, queries, new_key, new_value, centroid_keys, centroid_values, key_cache, value_cache)


def project_kernel(parts, weight, out):
    rows = parts.shape[1] // 2
    half = parts.shape[2] // 2
    weighted = parts[:, :rows, :]
    peak = parts[:, rows:, 0:1]
    total = parts[:, rows:, half : half + 1]
    scale = jnp.exp(peak - jnp.max(peak, axis=0, keepdims=True))
    total = jnp.sum(total * scale, axis=0)
    attended = (jnp.sum(weighted * scale, axis=0) / total).astype(jnp.bfloat16)
    seq_count = out.shape[0]
    sums = None
    for g in range(weight.shape[0]):
        term = jnp.dot(
            attended[g * seq_count : (g + 1) * seq_count],
            weight[g, 0],
            preferred_element_type=jnp.float32,
        )
        sums = term if sums is None else sums + term
    out[...] = sums.astype(jnp.bfloat16)


def project(parts, weight):
    seq_count = parts.shape[1] // (2 * weight.shape[0])
    return pl.pallas_call(
        project_kernel,
        out_shape=jax.ShapeDtypeStruct((seq_count, weight.shape[3]), jnp.bfloat16),
        in_specs=[VMEM_SPEC, VMEM_SPEC],
        out_specs=VMEM_SPEC,
        compiler_params=pltpu.CompilerParams(vmem_limit_bytes=8 << 20),
    )(parts, weight)


def experts_kernel(
    blocks, chunks, x0, x1, x2, x3, gate_up, down, out, gate_up_held, down_held, spread, sem_up, sem_down
):
    block_rows, model_dim = x0.shape
    rows = 4 * block_rows
    tiles = gate_up.shape[3] // 128
    part = model_dim // chunks
    width = 1024
    exp_pos = lax.axis_index("exp")

    def up_copy(c, t):
        return pltpu.make_async_copy(
            gate_up.at[0, pl.ds(c * part, part), :, pl.ds(t * 128, 128)],
            gate_up_held.at[t, pl.ds(c * part, part)],
            sem_up.at[c, t],
        )

    def down_copy(j):
        return pltpu.make_async_copy(
            down.at[0, :, pl.ds(j * width, width)],
            down_held.at[:, pl.ds(j * width, width)],
            sem_down.at[j],
        )

    for c in range(chunks):
        for t in range(tiles):
            up_copy(c, t).start()
    for j in range(model_dim // width):
        down_copy(j).start()
    source = lax.broadcasted_iota(jnp.int32, (128, 256), 0)
    target = lax.broadcasted_iota(jnp.int32, (128, 256), 1)
    to_even = jnp.where(target == 2 * source, 1.0, 0.0).astype(jnp.bfloat16)
    to_odd = jnp.where(target == 2 * source + 1, 1.0, 0.0).astype(jnp.bfloat16)
    for k in range(model_dim // 128):
        piece = jnp.concatenate([x[:, k * 128 : (k + 1) * 128] for x in (x0, x1, x2, x3)], axis=0)
        columns = slice(k * 256, (k + 1) * 256)
        spread[0:rows, columns] = jnp.dot(
            piece, to_even, preferred_element_type=jnp.float32
        ).astype(jnp.bfloat16)
        spread[rows : 2 * rows, columns] = jnp.dot(
            piece, to_odd, preferred_element_type=jnp.float32
        ).astype(jnp.bfloat16)
    flat = gate_up_held.reshape(tiles, 2 * model_dim, 128)
    sums = [jnp.zeros((2 * rows, 256), jnp.float32) for _ in range(tiles // 2)]
    for c in range(chunks):
        for t in range(tiles):
            up_copy(c, t).wait()
        left = spread[:, c * 2 * part : (c + 1) * 2 * part]
        here = pl.ds(c * 2 * part, 2 * part)
        for u in range(tiles // 2):
            right = jnp.concatenate([flat[2 * u, here, :], flat[2 * u + 1, here, :]], axis=1)
            sums[u] = sums[u] + jnp.dot(left, right, preferred_element_type=jnp.float32)
    both = jnp.concatenate(sums, axis=1)
    gate, up = both[:rows], both[rows:]
    activated = (jax.nn.silu(gate) * up).astype(jnp.bfloat16)
    for j in range(model_dim // width):
        down_copy(j).wait()
        for q in range(width // 256):
            b = j * (width // 256) + q
            result = jnp.dot(
                activated, down_held[:, b * 256 : (b + 1) * 256], preferred_element_type=jnp.float32
            )
            for i in range(blocks):
                seq_count = rows // blocks
                piece = result[i * seq_count : (i + 1) * seq_count].astype(jnp.bfloat16)
                out[b * blocks + lax.bitwise_xor(exp_pos, i)] = piece


def experts(pieces, gate_up, down, blocks):
    block_rows, model_dim = pieces[0].shape
    rows = 4 * block_rows
    hidden = down.shape[1]
    tiles = hidden // 128
    chunks = 8
    return pl.pallas_call(
        functools.partial(experts_kernel, blocks, chunks),
        out_shape=jax.ShapeDtypeStruct(
            (model_dim // 256 * blocks, rows // blocks, 256), jnp.bfloat16
        ),
        in_specs=[VMEM_SPEC] * 4 + [ANY_SPEC] * 2,
        out_specs=VMEM_SPEC,
        scratch_shapes=[
            pltpu.VMEM((tiles, model_dim, 2, 128), jnp.bfloat16),
            pltpu.VMEM((hidden, model_dim), jnp.bfloat16),
            pltpu.VMEM((2 * rows, 2 * model_dim), jnp.bfloat16),
            pltpu.SemaphoreType.DMA((chunks, tiles)),
            pltpu.SemaphoreType.DMA((model_dim // 1024,)),
        ],
        compiler_params=pltpu.CompilerParams(vmem_limit_bytes=28 << 20),
    )(*pieces, gate_up, down)


def swapped(value, axes, count, mask):
    return lax.ppermute(value, axes, [(i, i ^ mask) for i in range(count)])


def body(
    queries,
    key_cache,
    value_cache,
    centroid_keys,
    centroid_values,
    selected,
    new_key,
    new_value,
    out_weight,
    residual,
    norm_gain,
    expert_ids,
    gate_weights,
    w_gate_up,
    w_down,
):
    ctx_devices = lax.axis_size("ctx")
    kvh_devices = lax.axis_size("kvh")
    exp_devices = lax.axis_size("exp")
    seq_count, model_dim = residual.shape
    plane = ctx_devices * kvh_devices

    parts = attention(
        queries, key_cache, value_cache, centroid_keys, centroid_values, selected, new_key, new_value
    )
    parts = lax.all_to_all(parts, "ctx", split_axis=0, concat_axis=0, tiled=True)
    projected = project(parts, out_weight)

    axes = ("ctx", "kvh")
    along_x = [swapped(projected, axes, plane, m) for m in (1, 2, 3)]
    sums = projected.astype(jnp.float32)
    for piece in along_x:
        sums = sums + piece.astype(jnp.float32)
    sums = sums.astype(jnp.bfloat16)
    along_z = [swapped(sums, axes, plane, m) for m in range(4, plane, 4)]
    sums = sums.astype(jnp.float32)
    for piece in along_z:
        sums = sums + piece.astype(jnp.float32)
    hidden1 = residual.astype(jnp.float32) + sums
    mean_square = jnp.mean(hidden1 * hidden1, axis=-1, keepdims=True)
    normed = (hidden1 * lax.rsqrt(mean_square + 1e-06) * norm_gain).astype(jnp.bfloat16)

    other = swapped(normed, "exp", exp_devices, 1)
    pair = jnp.concatenate([normed, other], axis=0)
    pieces = [pair] + [swapped(pair, "exp", exp_devices, m) for m in range(2, exp_devices, 2)]
    results = experts(pieces, w_gate_up, w_down, exp_devices)
    returned = lax.all_to_all(
        results, ("ctx", "kvh", "exp"), split_axis=0, concat_axis=0, tiled=True
    )

    expert = jnp.arange(ctx_devices * exp_devices, dtype=jnp.int32)
    matches = expert_ids[:, :, None] == expert[None, None, :]
    weight = jnp.sum(jnp.where(matches, gate_weights[:, :, None], 0.0), axis=1)
    weight = weight.T.reshape(ctx_devices, 1, exp_devices, seq_count)
    weight = jnp.broadcast_to(weight, (ctx_devices, kvh_devices, exp_devices, seq_count))
    weight = weight.reshape(ctx_devices * kvh_devices * exp_devices, seq_count, 1)
    expert_mix = jnp.sum(returned.astype(jnp.float32) * weight, axis=0)
    slice_width = expert_mix.shape[1]
    own_slice = lax.dynamic_slice_in_dim(
        hidden1, lax.axis_index(("ctx", "kvh")) * slice_width, slice_width, 1
    )
    return (own_slice + expert_mix).astype(jnp.bfloat16)


def solution(mesh):
    in_specs = (
        P("exp", "kvh", None, None),
        P("exp", "ctx", "kvh", None),
        P("exp", "ctx", "kvh", None),
        P("exp", "ctx", "kvh", None),
        P("exp", "ctx", "kvh", None),
        P("exp", "kvh", "ctx"),
        P("exp", "kvh", None),
        P("exp", "kvh", None),
        P("kvh", "ctx", None, None),
        P("exp", None),
        P(),
        P("exp", None),
        P("exp", None),
        P(("ctx", "exp"), None, None, "kvh"),
        P(("ctx", "exp"), "kvh", None),
    )
    out_specs = P("exp", ("ctx", "kvh"))
    return jax.shard_map(body, mesh=mesh, in_specs=in_specs, out_specs=out_specs, check_vma=False)
```

```python
import functools
import math

import jax
import jax.numpy as jnp
from jax import lax
from jax.experimental import pallas as pl
from jax.experimental.pallas import tpu as pltpu
from jax.sharding import PartitionSpec as P

VMEM_SPEC = pl.BlockSpec(memory_space=pltpu.VMEM)
SMEM_SPEC = pl.BlockSpec(memory_space=pltpu.SMEM)
ANY_SPEC = pl.BlockSpec(memory_space=pl.ANY)
MASKED = -1e30


def in_hbm(value):
    return pltpu.with_memory_space_constraint(value, pltpu.HBM)


def attention_kernel(
    selected_in,
    queries_in,
    new_key_in,
    new_value_in,
    centroid_keys,
    centroid_values,
    key_cache,
    value_cache,
    weight_in,
    out,
    weight_out,
    selected,
    queries,
    new_key,
    new_value,
    keys,
    values,
    small_sem,
    picked_sem,
):
    seq_count, heads_kv, query_count, head_dim = queries.shape
    clusters = centroid_keys.shape[1]
    sel_count = selected.shape[1]
    block_len = key_cache.shape[1] // clusters
    ctx_pos = lax.axis_index("ctx")
    pairs = (
        (selected_in, selected),
        (centroid_keys, keys.at[:, pl.ds(0, clusters)]),
        (queries_in, queries),
        (new_key_in, new_key),
        (new_value_in, new_value),
        (centroid_values, values.at[:, pl.ds(0, clusters)]),
        (weight_in, weight_out),
    )
    small = [
        pltpu.make_async_copy(source, held, small_sem.at[i]) for i, (source, held) in enumerate(pairs)
    ]
    for copy in small:
        copy.start()
    small[0].wait()
    picked = []
    for which, (source, held) in enumerate(((key_cache, keys), (value_cache, values))):
        for s in range(seq_count):
            for g in range(heads_kv):
                for j in range(sel_count):
                    block = selected[g, j, s] - ctx_pos * clusters
                    place = clusters + (g * sel_count + j) * block_len
                    picked.append(
                        pltpu.make_async_copy(
                            source.at[s, pl.ds(block * block_len, block_len)],
                            held.at[s, pl.ds(place, block_len)],
                            picked_sem.at[which, s, g * sel_count + j],
                        )
                    )
    for copy in picked:
        copy.start()
    for copy in small[1:6]:
        copy.wait()
    for copy in picked:
        copy.wait()
    positions = keys.shape[1]
    rows = positions * heads_kv
    flat_keys = keys.reshape(seq_count, rows, head_dim)
    flat_values = values.reshape(seq_count, rows, head_dim)
    shape = (heads_kv * query_count, rows)
    head_of_query = lax.broadcasted_iota(jnp.int32, shape, 0) // query_count
    column = lax.broadcasted_iota(jnp.int32, shape, 1)
    head_of_row = column % heads_kv
    position = column // heads_kv
    head_of_block = (position - clusters) // (sel_count * block_len)
    valid = (head_of_row == head_of_query) & (
        (position < clusters) | (head_of_block == head_of_query)
    )
    score_scale = 1.0 / math.sqrt(head_dim)
    for s in range(seq_count):
        query = queries[s].reshape(heads_kv * query_count, head_dim)
        scores = lax.dot_general(
            query, flat_keys[s], (((1,), (1,)), ((), ())), preferred_element_type=jnp.float32
        )
        scores = jnp.where(valid, scores * score_scale, MASKED)
        own = jnp.sum(
            queries[s].astype(jnp.float32) * new_key[s].astype(jnp.float32)[:, None, :],
            axis=-1,
            keepdims=True,
        ).reshape(heads_kv * query_count, 1)
        own = jnp.where(ctx_pos == 0, own * score_scale, MASKED)
        peak = jnp.maximum(jnp.max(scores, axis=-1, keepdims=True), own)
        probs = jnp.exp(scores - peak)
        own_prob = jnp.exp(own - peak)
        total = jnp.sum(probs, axis=-1, keepdims=True) + own_prob
        weighted = jnp.dot(
            probs.astype(jnp.bfloat16), flat_values[s], preferred_element_type=jnp.float32
        )
        own_value = jnp.broadcast_to(
            new_value[s].astype(jnp.float32)[:, None, :], (heads_kv, query_count, head_dim)
        ).reshape(heads_kv * query_count, head_dim)
        weighted = weighted + own_prob * own_value
        lane = lax.broadcasted_iota(jnp.int32, weighted.shape, 1)
        stats = jnp.where(lane < head_dim // 2, peak, total)
        for g in range(heads_kv):
            part = slice(g * query_count, (g + 1) * query_count)
            out[:, g * seq_count + s, :] = weighted[part]
            out[:, (heads_kv + g) * seq_count + s, :] = stats[part]
    small[6].wait()


def attention(
    queries, key_cache, value_cache, centroid_keys, centroid_values, selected, new_key, new_value, weight
):
    seq_count, heads_kv, query_count, head_dim = queries.shape
    clusters = centroid_keys.shape[1]
    sel_count = selected.shape[2]
    selected = selected.transpose(1, 2, 0)
    block_len = key_cache.shape[1] // clusters
    held = pltpu.VMEM(
        (seq_count, clusters + heads_kv * sel_count * block_len, heads_kv, head_dim), jnp.bfloat16
    )
    operands = (
        selected, queries, new_key, new_value, centroid_keys, centroid_values, key_cache, value_cache, weight
    )
    return pl.pallas_call(
        attention_kernel,
        out_shape=(
            pltpu.VMEM((query_count, 2 * heads_kv * seq_count, head_dim), jnp.float32),
            pltpu.VMEM(weight.shape, weight.dtype),
        ),
        in_specs=[ANY_SPEC] * 9,
        out_specs=(VMEM_SPEC, VMEM_SPEC),
        scratch_shapes=[
            pltpu.SMEM(selected.shape, selected.dtype),
            pltpu.VMEM(queries.shape, queries.dtype),
            pltpu.VMEM(new_key.shape, new_key.dtype),
            pltpu.VMEM(new_value.shape, new_value.dtype),
            held,
            held,
            pltpu.SemaphoreType.DMA((7,)),
            pltpu.SemaphoreType.DMA((2, seq_count, heads_kv * sel_count)),
        ],
        compiler_params=pltpu.CompilerParams(vmem_limit_bytes=12 << 20),
    )(*[in_hbm(operand) for operand in operands])


def project_kernel(parts, weight, before, out):
    rows = parts.shape[1] // 2
    half = parts.shape[2] // 2
    weighted = parts[:, :rows, :]
    peak = parts[:, rows:, 0:1]
    total = parts[:, rows:, half : half + 1]
    scale = jnp.exp(peak - jnp.max(peak, axis=0, keepdims=True))
    total = jnp.sum(total * scale, axis=0)
    attended = (jnp.sum(weighted * scale, axis=0) / total).astype(jnp.bfloat16)
    seq_count = out.shape[0]
    sums = None
    for g in range(weight.shape[0]):
        term = jnp.dot(
            attended[g * seq_count : (g + 1) * seq_count],
            weight[g, 0],
            preferred_element_type=jnp.float32,
        )
        sums = term if sums is None else sums + term
    out[...] = sums.astype(jnp.bfloat16)


def project(parts, weight, before):
    seq_count = parts.shape[1] // (2 * weight.shape[0])
    return pl.pallas_call(
        project_kernel,
        out_shape=jax.ShapeDtypeStruct((seq_count, weight.shape[3]), jnp.bfloat16),
        in_specs=[VMEM_SPEC, VMEM_SPEC, ANY_SPEC],
        out_specs=VMEM_SPEC,
        compiler_params=pltpu.CompilerParams(vmem_limit_bytes=8 << 20),
    )(parts, weight, before)


def fetch_kernel(first, source, *refs):
    out, sem = refs[-2:]
    count = out.shape[0]
    chunks = 4
    part = source.shape[1] // chunks
    copies = [
        pltpu.make_async_copy(
            source.at[0, pl.ds(c * part, part), :, pl.ds((first + t) * 128, 128)],
            out.at[t, pl.ds(c * part, part)],
            sem.at[t, c],
        )
        for c in range(chunks)
        for t in range(count)
    ]
    for copy in copies:
        copy.start()
    for copy in copies:
        copy.wait()


def fetch(weights, first, count, *after):
    depth = weights.shape[1]
    tiles = pl.pallas_call(
        functools.partial(fetch_kernel, first),
        out_shape=pltpu.VMEM((count, depth, 2, 128), weights.dtype),
        in_specs=[ANY_SPEC] * (1 + len(after)),
        out_specs=VMEM_SPEC,
        scratch_shapes=[pltpu.SemaphoreType.DMA((count, 4))],
        compiler_params=pltpu.CompilerParams(vmem_limit_bytes=1 << 20),
        cost_estimate=pl.CostEstimate(
            flops=0, bytes_accessed=count * depth * 512, transcendentals=0
        ),
    )(in_hbm(weights), *after)
    return tiles.reshape(count, 2 * depth, 128)


def experts_kernel(blocks, x0, x1, x2, x3, *refs):
    *tiles, down, out, spread = refs
    block_rows, model_dim = x0.shape
    rows = 4 * block_rows
    seq_count = rows // blocks
    exp_pos = lax.axis_index("exp")
    source = lax.broadcasted_iota(jnp.int32, (128, 512), 0)
    target = lax.broadcasted_iota(jnp.int32, (128, 512), 1)
    ends = (target == 2 * source) | (target == 2 * source + 257)
    to_both = jnp.where(ends, 1.0, 0.0).astype(jnp.bfloat16)
    group = 8

    def spread_group(k, carry):
        pieces = []
        for j in range(group):
            columns = pl.ds(pl.multiple_of((k * group + j) * 128, 128), 128)
            pieces += [x[:, columns] for x in (x0, x1, x2, x3)]
        result = jnp.dot(
            jnp.concatenate(pieces, axis=0), to_both, preferred_element_type=jnp.float32
        ).astype(jnp.bfloat16)
        for j in range(group):
            columns = pl.ds(pl.multiple_of((k * group + j) * 256, 256), 256)
            spread[0:rows, columns] = result[j * rows : (j + 1) * rows, 0:256]
            spread[rows : 2 * rows, columns] = result[j * rows : (j + 1) * rows, 256:512]
        return carry

    lax.fori_loop(0, model_dim // 128 // group, spread_group, 0)
    lanes = [tile.at[t] for tile in tiles for t in range(tile.shape[0])]
    depth = 1024
    both = []
    for u in range(len(lanes) // 2):
        total = jnp.zeros((2 * rows, 256), jnp.float32)
        for c in range(2 * model_dim // depth):
            here = slice(c * depth, (c + 1) * depth)
            right = jnp.concatenate([lanes[2 * u][here, :], lanes[2 * u + 1][here, :]], axis=1)
            total = total + jnp.dot(spread[:, here], right, preferred_element_type=jnp.float32)
        both.append(total)
    both = jnp.concatenate(both, axis=1)
    gate, up = both[:rows], both[rows:]
    activated = (jax.nn.silu(gate) * up).astype(jnp.bfloat16)
    width = 512

    def down_part(b, carry):
        columns = pl.ds(pl.multiple_of(b * width, width), width)
        result = jnp.dot(
            activated, down[0, :, columns], preferred_element_type=jnp.float32
        ).astype(jnp.bfloat16)
        for q in range(width // 256):
            for i in range(blocks):
                place = (b * (width // 256) + q) * blocks + lax.bitwise_xor(exp_pos, i)
                out[place] = result[i * seq_count : (i + 1) * seq_count, q * 256 : (q + 1) * 256]
        return carry

    lax.fori_loop(0, model_dim // width, down_part, 0)


def experts(pieces, tiles, down, blocks):
    block_rows, model_dim = pieces[0].shape
    rows = 4 * block_rows
    return pl.pallas_call(
        functools.partial(experts_kernel, blocks),
        out_shape=pltpu.VMEM((model_dim // 256 * blocks, rows // blocks, 256), jnp.bfloat16),
        in_specs=[VMEM_SPEC] * (5 + len(tiles)),
        out_specs=VMEM_SPEC,
        scratch_shapes=[pltpu.VMEM((2 * rows, 2 * model_dim), jnp.bfloat16)],
        compiler_params=pltpu.CompilerParams(vmem_limit_bytes=16 << 20),
    )(*pieces, *tiles, down)


def sum_kernel(p0, p1, p2, p3, before, out):
    total = p0[...].astype(jnp.float32)
    for piece in (p1, p2, p3):
        total = total + piece[...].astype(jnp.float32)
    out[...] = total.astype(out.dtype)


def sum_pieces(pieces, before):
    return pl.pallas_call(
        sum_kernel,
        out_shape=pltpu.VMEM(pieces[0].shape, pieces[0].dtype),
        in_specs=[VMEM_SPEC] * 4 + [ANY_SPEC],
        out_specs=VMEM_SPEC,
        compiler_params=pltpu.CompilerParams(vmem_limit_bytes=2 << 20),
    )(*pieces, before)


def norm_kernel(p0, p1, p2, p3, residual, gain, before, hidden, normed):
    total = residual[...].astype(jnp.float32)
    for piece in (p0, p1, p2, p3):
        total = total + piece[...].astype(jnp.float32)
    mean_square = jnp.mean(total * total, axis=-1, keepdims=True)
    hidden[...] = total
    normed[...] = (total * lax.rsqrt(mean_square + 1e-06) * gain[...]).astype(normed.dtype)


def norm(pieces, residual, gain, before):
    shape = residual.shape
    return pl.pallas_call(
        norm_kernel,
        out_shape=(pltpu.VMEM(shape, jnp.float32), pltpu.VMEM(shape, jnp.bfloat16)),
        in_specs=[VMEM_SPEC] * 6 + [ANY_SPEC],
        out_specs=(VMEM_SPEC, VMEM_SPEC),
        compiler_params=pltpu.CompilerParams(vmem_limit_bytes=2 << 20),
    )(*pieces, residual, gain.reshape(1, -1), before)


def swapped(value, axes, count, mask):
    return lax.ppermute(value, axes, [(i, i ^ mask) for i in range(count)])


def body(
    queries,
    key_cache,
    value_cache,
    centroid_keys,
    centroid_values,
    selected,
    new_key,
    new_value,
    out_weight,
    residual,
    norm_gain,
    expert_ids,
    gate_weights,
    w_gate_up,
    w_down,
):
    ctx_devices = lax.axis_size("ctx")
    kvh_devices = lax.axis_size("kvh")
    exp_devices = lax.axis_size("exp")
    seq_count, model_dim = residual.shape
    plane = ctx_devices * kvh_devices

    parts, out_weight = attention(
        queries,
        key_cache,
        value_cache,
        centroid_keys,
        centroid_values,
        selected,
        new_key,
        new_value,
        out_weight,
    )
    parts = lax.all_to_all(parts, "ctx", split_axis=0, concat_axis=0, tiled=True)

    device = jnp.arange(plane * exp_devices, dtype=jnp.int32)
    expert = device // (kvh_devices * exp_devices) * exp_devices + device % exp_devices
    matches = expert_ids.T[:, None, :] == expert[None, :, None]
    weight = jnp.sum(jnp.where(matches, gate_weights.T[:, None, :], 0.0), axis=0)
    projected = project(parts, out_weight, weight)

    axes = ("ctx", "kvh")
    along_x = [projected] + [swapped(projected, axes, plane, m) for m in (1, 2, 3)]
    tiles = [fetch(w_gate_up, 0, 2, projected)]
    sums = sum_pieces(along_x, tiles[0])
    along_z = [sums] + [swapped(sums, axes, plane, m) for m in range(4, plane, 4)]
    tiles.append(fetch(w_gate_up, 2, 2, sums))
    hidden1, normed = norm(along_z, residual, norm_gain, tiles[1])

    other = swapped(normed, "exp", exp_devices, 1)
    pair = jnp.concatenate([normed, other], axis=0)
    tiles.append(fetch(w_gate_up, 4, 2, pair))
    pieces = [pair] + [swapped(pair, "exp", exp_devices, m) for m in range(2, exp_devices, 2)]
    results = experts(pieces, tiles, w_down, exp_devices)
    returned = lax.all_to_all(
        results, ("ctx", "kvh", "exp"), split_axis=0, concat_axis=0, tiled=True
    )

    expert_mix = jnp.sum(returned.astype(jnp.float32) * weight[:, :, None], axis=0)
    slice_width = expert_mix.shape[1]
    own_slice = lax.dynamic_slice_in_dim(
        hidden1, lax.axis_index(("ctx", "kvh")) * slice_width, slice_width, 1
    )
    return (own_slice + expert_mix).astype(jnp.bfloat16)


def solution(mesh):
    in_specs = (
        P("exp", "kvh", None, None),
        P("exp", "ctx", "kvh", None),
        P("exp", "ctx", "kvh", None),
        P("exp", "ctx", "kvh", None),
        P("exp", "ctx", "kvh", None),
        P("exp", "kvh", "ctx"),
        P("exp", "kvh", None),
        P("exp", "kvh", None),
        P("kvh", "ctx", None, None),
        P("exp", None),
        P(),
        P("exp", None),
        P("exp", None),
        P(("ctx", "exp"), None, None, "kvh"),
        P(("ctx", "exp"), "kvh", None),
    )
    out_specs = P("exp", ("ctx", "kvh"))
    return jax.shard_map(body, mesh=mesh, in_specs=in_specs, out_specs=out_specs, check_vma=False)
```

```python
import functools
import math

import jax
import jax.numpy as jnp
from jax import lax
from jax.experimental import pallas as pl
from jax.experimental.pallas import tpu as pltpu
from jax.sharding import PartitionSpec as P

VMEM_SPEC = pl.BlockSpec(memory_space=pltpu.VMEM)
SMEM_SPEC = pl.BlockSpec(memory_space=pltpu.SMEM)
ANY_SPEC = pl.BlockSpec(memory_space=pl.ANY)
MASKED = -1e30


def in_hbm(value):
    return pltpu.with_memory_space_constraint(value, pltpu.HBM)


def attention_kernel(
    selected_in,
    queries_in,
    new_key_in,
    new_value_in,
    centroid_keys,
    centroid_values,
    key_cache,
    value_cache,
    weight_in,
    out,
    weight_out,
    selected,
    queries,
    new_key,
    new_value,
    keys,
    values,
    small_sem,
    picked_sem,
):
    seq_count, heads_kv, query_count, head_dim = queries.shape
    centroid_rows = centroid_keys.shape[1]
    clusters = centroid_rows // heads_kv
    sel_count = selected.shape[1]
    block_rows = key_cache.shape[1] // clusters
    ctx_pos = lax.axis_index("ctx")
    pairs = (
        (selected_in, selected),
        (centroid_keys, keys.at[:, pl.ds(0, centroid_rows)]),
        (queries_in, queries),
        (new_key_in, new_key),
        (new_value_in, new_value),
        (centroid_values, values.at[:, pl.ds(0, centroid_rows)]),
        (weight_in, weight_out),
    )
    small = [
        pltpu.make_async_copy(source, held, small_sem.at[i]) for i, (source, held) in enumerate(pairs)
    ]
    for copy in small[:6]:
        copy.start()
    small[0].wait()
    picked = ([], [])
    for which, (source, held) in enumerate(((key_cache, keys), (value_cache, values))):
        for s in range(seq_count):
            for g in range(heads_kv):
                for j in range(sel_count):
                    block = selected[g, j, s] - ctx_pos * clusters
                    start = pl.multiple_of(block * block_rows, block_rows)
                    place = centroid_rows + (g * sel_count + j) * block_rows
                    copy = pltpu.make_async_copy(
                        source.at[s, pl.ds(start, block_rows)],
                        held.at[s, pl.ds(place, block_rows)],
                        picked_sem.at[which, s, g * sel_count + j],
                    )
                    copy.start()
                    picked[which].append(copy)
    small[6].start()
    for copy in small[1:4] + picked[0]:
        copy.wait()
    rows = keys.shape[1]
    heads = heads_kv * query_count
    shape = (seq_count * heads, rows)
    head_of_query = lax.broadcasted_iota(jnp.int32, shape, 0) // query_count % heads_kv
    column = lax.broadcasted_iota(jnp.int32, shape, 1)
    head_of_block = (column - centroid_rows) // (sel_count * block_rows)
    valid = (column % heads_kv == head_of_query) & (
        (column < centroid_rows) | (head_of_block == head_of_query)
    )
    score_scale = 1.0 / math.sqrt(head_dim)
    scores, own = [], []
    for s in range(seq_count):
        scores.append(
            lax.dot_general(
                queries[s].reshape(heads, head_dim),
                keys[s],
                (((1,), (1,)), ((), ())),
                preferred_element_type=jnp.float32,
            )
        )
        products = queries[s].astype(jnp.float32) * new_key[s].astype(jnp.float32)[:, None, :]
        own.append(jnp.sum(products, axis=-1, keepdims=True).reshape(heads, 1))
    scores = jnp.where(valid, jnp.concatenate(scores, axis=0) * score_scale, MASKED)
    own = jnp.where(ctx_pos == 0, jnp.concatenate(own, axis=0) * score_scale, MASKED)
    peak = jnp.maximum(jnp.max(scores, axis=-1, keepdims=True), own)
    probs = jnp.exp(scores - peak)
    own_prob = jnp.exp(own - peak)
    total = jnp.sum(probs, axis=-1, keepdims=True) + own_prob
    probs = probs.astype(jnp.bfloat16)
    lane = lax.broadcasted_iota(jnp.int32, (seq_count * heads, head_dim), 1)
    stats = jnp.where(lane < head_dim // 2, peak, total)
    for copy in small[4:6] + picked[1]:
        copy.wait()
    for s in range(seq_count):
        mine = slice(s * heads, (s + 1) * heads)
        weighted = jnp.dot(probs[mine], values[s], preferred_element_type=jnp.float32)
        own_value = jnp.broadcast_to(
            new_value[s].astype(jnp.float32)[:, None, :], (heads_kv, query_count, head_dim)
        ).reshape(heads, head_dim)
        weighted = weighted + own_prob[mine] * own_value
        for g in range(heads_kv):
            part = slice(g * query_count, (g + 1) * query_count)
            out[:, g * seq_count + s, :] = weighted[part]
            out[:, (heads_kv + g) * seq_count + s, :] = stats[mine][part]
    small[6].wait()


def attention(
    queries, key_cache, value_cache, centroid_keys, centroid_values, selected, new_key, new_value, weight
):
    seq_count, heads_kv, query_count, head_dim = queries.shape
    clusters = centroid_keys.shape[1]
    sel_count = selected.shape[2]
    block_rows = key_cache.shape[1] // clusters * heads_kv
    selected = selected.transpose(1, 2, 0)
    centroid_keys, centroid_values, key_cache, value_cache = (
        value.reshape(seq_count, -1, head_dim)
        for value in (centroid_keys, centroid_values, key_cache, value_cache)
    )
    held_rows = clusters * heads_kv + heads_kv * sel_count * block_rows
    held = pltpu.VMEM((seq_count, held_rows, head_dim), jnp.bfloat16)
    operands = (
        selected, queries, new_key, new_value, centroid_keys, centroid_values, key_cache, value_cache, weight
    )
    return pl.pallas_call(
        attention_kernel,
        out_shape=(
            pltpu.VMEM((query_count, 2 * heads_kv * seq_count, head_dim), jnp.float32),
            pltpu.VMEM(weight.shape, weight.dtype),
        ),
        in_specs=[ANY_SPEC] * 9,
        out_specs=(VMEM_SPEC, VMEM_SPEC),
        scratch_shapes=[
            pltpu.SMEM(selected.shape, selected.dtype),
            pltpu.VMEM(queries.shape, queries.dtype),
            pltpu.VMEM(new_key.shape, new_key.dtype),
            pltpu.VMEM(new_value.shape, new_value.dtype),
            held,
            held,
            pltpu.SemaphoreType.DMA((7,)),
            pltpu.SemaphoreType.DMA((2, seq_count, heads_kv * sel_count)),
        ],
        compiler_params=pltpu.CompilerParams(vmem_limit_bytes=12 << 20),
    )(*[in_hbm(operand) for operand in operands])


def project_kernel(parts, weight, out):
    rows = parts.shape[1] // 2
    half = parts.shape[2] // 2
    weighted = parts[:, :rows, :]
    peak = parts[:, rows:, 0:1]
    total = parts[:, rows:, half : half + 1]
    scale = jnp.exp(peak - jnp.max(peak, axis=0, keepdims=True))
    total = jnp.sum(total * scale, axis=0)
    attended = (jnp.sum(weighted * scale, axis=0) / total).astype(jnp.bfloat16)
    seq_count = out.shape[0]
    sums = None
    for g in range(weight.shape[0]):
        term = jnp.dot(
            attended[g * seq_count : (g + 1) * seq_count],
            weight[g, 0],
            preferred_element_type=jnp.float32,
        )
        sums = term if sums is None else sums + term
    out[...] = sums.astype(jnp.bfloat16)


def project(parts, weight):
    seq_count = parts.shape[1] // (2 * weight.shape[0])
    return pl.pallas_call(
        project_kernel,
        out_shape=jax.ShapeDtypeStruct((seq_count, weight.shape[3]), jnp.bfloat16),
        in_specs=[VMEM_SPEC, VMEM_SPEC],
        out_specs=VMEM_SPEC,
        compiler_params=pltpu.CompilerParams(vmem_limit_bytes=8 << 20),
    )(parts, weight)


def fetch_kernel(first, source, *refs):
    out, sem = refs[-2:]
    count = out.shape[0]
    chunks = 4
    part = source.shape[1] // chunks
    copies = [
        pltpu.make_async_copy(
            source.at[0, pl.ds(c * part, part), :, pl.ds((first + t) * 128, 128)],
            out.at[t, pl.ds(c * part, part)],
            sem.at[t, c],
        )
        for c in range(chunks)
        for t in range(count)
    ]
    for copy in copies:
        copy.start()
    for copy in copies:
        copy.wait()


def fetch(weights, first, count, *after):
    depth = weights.shape[1]
    tiles = pl.pallas_call(
        functools.partial(fetch_kernel, first),
        out_shape=pltpu.VMEM((count, depth, 2, 128), weights.dtype),
        in_specs=[ANY_SPEC] * (1 + len(after)),
        out_specs=VMEM_SPEC,
        scratch_shapes=[pltpu.SemaphoreType.DMA((count, 4))],
        compiler_params=pltpu.CompilerParams(vmem_limit_bytes=1 << 20),
        cost_estimate=pl.CostEstimate(
            flops=0, bytes_accessed=count * depth * 512, transcendentals=0
        ),
    )(in_hbm(weights), *after)
    return tiles.reshape(count, 2 * depth, 128)


def experts_kernel(order, x0, x1, *refs):
    *tiles, down, out, spread = refs
    half, model_dim = x0.shape
    rows = 2 * half
    blocks = len(order)
    seq_count = rows // blocks
    exp_pos = lax.axis_index("exp")
    source = lax.broadcasted_iota(jnp.int32, (128, 512), 0)
    target = lax.broadcasted_iota(jnp.int32, (128, 512), 1)
    ends = (target == 2 * source) | (target == 2 * source + 257)
    to_both = jnp.where(ends, 1.0, 0.0).astype(jnp.bfloat16)
    pieces = []
    for j in range(model_dim // 128):
        pieces += [x[:, j * 128 : (j + 1) * 128] for x in (x0, x1)]
    result = jnp.dot(
        jnp.concatenate(pieces, axis=0), to_both, preferred_element_type=jnp.float32
    ).astype(jnp.bfloat16)
    for j in range(model_dim // 128):
        columns = slice(j * 256, (j + 1) * 256)
        spread[0:rows, columns] = result[j * rows : (j + 1) * rows, 0:256]
        spread[rows : 2 * rows, columns] = result[j * rows : (j + 1) * rows, 256:512]
    lanes = [tile.at[t] for tile in tiles for t in range(tile.shape[0])]
    depth = 1024
    both = []
    for u in range(len(lanes) // 2):
        total = jnp.zeros((2 * rows, 256), jnp.float32)
        for c in range(2 * model_dim // depth):
            here = slice(c * depth, (c + 1) * depth)
            right = jnp.concatenate([lanes[2 * u][here, :], lanes[2 * u + 1][here, :]], axis=1)
            total = total + jnp.dot(spread[:, here], right, preferred_element_type=jnp.float32)
        both.append(total)
    both = jnp.concatenate(both, axis=1)
    gate, up = both[:rows], both[rows:]
    activated = (jax.nn.silu(gate) * up).astype(jnp.bfloat16)
    width = 1024

    def down_part(b, carry):
        columns = pl.ds(pl.multiple_of(b * width, width), width)
        result = jnp.dot(
            activated, down[0, :, columns], preferred_element_type=jnp.float32
        ).astype(jnp.bfloat16)
        for q in range(width // 256):
            for p, i in enumerate(order):
                place = (b * (width // 256) + q) * blocks + lax.bitwise_xor(exp_pos, i)
                mine = result[p * seq_count : (p + 1) * seq_count]
                out[place, 0:seq_count] = mine[:, q * 256 : q * 256 + 128]
                out[place, seq_count : 2 * seq_count] = mine[:, q * 256 + 128 : (q + 1) * 256]
        return carry

    lax.fori_loop(0, model_dim // width, down_part, 0)


def experts(pieces, tiles, down, order):
    half, model_dim = pieces[0].shape
    rows = 2 * half
    blocks = len(order)
    return pl.pallas_call(
        functools.partial(experts_kernel, order),
        out_shape=pltpu.VMEM((model_dim // 256 * blocks, 2 * rows // blocks, 128), jnp.bfloat16),
        in_specs=[VMEM_SPEC] * (3 + len(tiles)),
        out_specs=VMEM_SPEC,
        scratch_shapes=[pltpu.VMEM((2 * rows, 2 * model_dim), jnp.bfloat16)],
        compiler_params=pltpu.CompilerParams(vmem_limit_bytes=16 << 20),
    )(*pieces, *tiles, down)


def sum_kernel(p0, p1, p2, p3, before, out):
    total = p0[...].astype(jnp.float32)
    for piece in (p1, p2, p3):
        total = total + piece[...].astype(jnp.float32)
    out[...] = total.astype(out.dtype)


def sum_pieces(pieces, before):
    return pl.pallas_call(
        sum_kernel,
        out_shape=pltpu.VMEM(pieces[0].shape, pieces[0].dtype),
        in_specs=[VMEM_SPEC] * 4 + [ANY_SPEC],
        out_specs=VMEM_SPEC,
        compiler_params=pltpu.CompilerParams(vmem_limit_bytes=2 << 20),
    )(*pieces, before)


def norm_kernel(sizes, p0, p1, p2, p3, residual, gain, ids, gates, before, own, normed, mix):
    kvh_devices, exp_devices = sizes
    seq_count = residual.shape[0]
    total = residual[...].astype(jnp.float32)
    for piece in (p0, p1, p2, p3):
        total = total + piece[...].astype(jnp.float32)
    mean_square = jnp.mean(total * total, axis=-1, keepdims=True)
    normed[...] = (total * lax.rsqrt(mean_square + 1e-06) * gain[...]).astype(normed.dtype)
    place = lax.axis_index("ctx") * kvh_devices + lax.axis_index("kvh")
    width = own.shape[1]
    own[...] = jnp.zeros(own.shape, own.dtype)
    for p in range(total.shape[1] // width):
        @pl.when(place == p)
        def _():
            own[...] = total[:, p * width : (p + 1) * width]

    shape = (2 * seq_count, mix.shape[1])
    column = lax.broadcasted_iota(jnp.int32, shape, 1)
    device = column // (2 * seq_count)
    expert = device // (kvh_devices * exp_devices) * exp_devices + device % exp_devices
    expert = jnp.where(
        column % (2 * seq_count) == lax.broadcasted_iota(jnp.int32, shape, 0), expert, -1
    )
    weight = jnp.zeros(shape, jnp.float32)
    both_ids = jnp.concatenate([ids[...], ids[...]], axis=0)
    both_gates = jnp.concatenate([gates[...], gates[...]], axis=0)
    for k in range(ids.shape[1]):
        weight = weight + jnp.where(both_ids[:, k : k + 1] == expert, both_gates[:, k : k + 1], 0.0)
    high = weight.astype(jnp.bfloat16)
    mix[0 : 2 * seq_count] = high
    mix[2 * seq_count : 4 * seq_count] = (weight - high.astype(jnp.float32)).astype(jnp.bfloat16)


def norm(pieces, residual, gain, ids, gates, before, sizes, devices):
    seq_count, model_dim = residual.shape
    columns = devices * 2 * seq_count
    return pl.pallas_call(
        functools.partial(norm_kernel, sizes),
        out_shape=(
            pltpu.VMEM((seq_count, 256), jnp.float32),
            pltpu.VMEM((seq_count, model_dim), jnp.bfloat16),
            pltpu.VMEM((4 * seq_count, columns), jnp.bfloat16),
        ),
        in_specs=[VMEM_SPEC] * 8 + [ANY_SPEC],
        out_specs=(VMEM_SPEC,) * 3,
        compiler_params=pltpu.CompilerParams(vmem_limit_bytes=2 << 20),
    )(*pieces, residual, gain.reshape(1, -1), ids, gates, before)


def stack_kernel(p0, p1, p2, p3, before, out):
    out[...] = jnp.concatenate([p0[...], p1[...], p2[...], p3[...]], axis=0)


def stack(pieces, before):
    rows, columns = pieces[0].shape
    return pl.pallas_call(
        stack_kernel,
        out_shape=pltpu.VMEM((4 * rows, columns), pieces[0].dtype),
        in_specs=[VMEM_SPEC] * 4 + [ANY_SPEC],
        out_specs=VMEM_SPEC,
        compiler_params=pltpu.CompilerParams(vmem_limit_bytes=2 << 20),
    )(*pieces, before)


def mix_kernel(returned, mix, own, out):
    seq_count = own.shape[0]
    sums = jnp.dot(mix[...], returned[...], preferred_element_type=jnp.float32)
    sums = sums[0 : 2 * seq_count] + sums[2 * seq_count : 4 * seq_count]
    width = sums.shape[1]
    out[:, 0:width] = (own[:, 0:width] + sums[0:seq_count]).astype(out.dtype)
    out[:, width : 2 * width] = (own[:, width : 2 * width] + sums[seq_count:]).astype(out.dtype)


def mix_results(returned, mix, own):
    return pl.pallas_call(
        mix_kernel,
        out_shape=jax.ShapeDtypeStruct(own.shape, jnp.bfloat16),
        in_specs=[VMEM_SPEC] * 3,
        out_specs=VMEM_SPEC,
        compiler_params=pltpu.CompilerParams(vmem_limit_bytes=2 << 20),
    )(returned.reshape(-1, returned.shape[2]), mix, own)


def swapped(value, axes, count, mask):
    return lax.ppermute(value, axes, [(i, i ^ mask) for i in range(count)])


def body(
    queries,
    key_cache,
    value_cache,
    centroid_keys,
    centroid_values,
    selected,
    new_key,
    new_value,
    out_weight,
    residual,
    norm_gain,
    expert_ids,
    gate_weights,
    w_gate_up,
    w_down,
):
    ctx_devices = lax.axis_size("ctx")
    kvh_devices = lax.axis_size("kvh")
    exp_devices = lax.axis_size("exp")
    plane = ctx_devices * kvh_devices

    parts, out_weight = attention(
        queries,
        key_cache,
        value_cache,
        centroid_keys,
        centroid_values,
        selected,
        new_key,
        new_value,
        out_weight,
    )
    parts = lax.all_to_all(parts, "ctx", split_axis=0, concat_axis=0, tiled=True)

    projected = project(parts, out_weight)

    axes = ("ctx", "kvh")
    along_x = [projected] + [swapped(projected, axes, plane, m) for m in (1, 2, 3)]
    tiles = [fetch(w_gate_up, 0, 2, projected)]
    sums = sum_pieces(along_x, tiles[0])
    along_z = [sums] + [swapped(sums, axes, plane, m) for m in range(4, plane, 4)]
    tiles.append(fetch(w_gate_up, 2, 2, sums))
    own, normed, mix = norm(
        along_z,
        residual,
        norm_gain,
        expert_ids,
        gate_weights,
        tiles[1],
        (kvh_devices, exp_devices),
        plane * exp_devices,
    )

    steps = range(0, exp_devices, 2)
    along_y = [normed] + [swapped(normed, "exp", exp_devices, m) for m in steps[1:]]
    tiles.append(fetch(w_gate_up, 4, 2, normed))
    mine = stack(along_y, tiles[2])
    other = swapped(mine, "exp", exp_devices, 1)
    order = tuple(steps) + tuple(m + 1 for m in steps)
    results = experts((mine, other), tiles, w_down, order)
    returned = lax.all_to_all(
        results, ("ctx", "kvh", "exp"), split_axis=0, concat_axis=0, tiled=True
    )
    return mix_results(returned, mix, own)


def solution(mesh):
    in_specs = (
        P("exp", "kvh", None, None),
        P("exp", "ctx", "kvh", None),
        P("exp", "ctx", "kvh", None),
        P("exp", "ctx", "kvh", None),
        P("exp", "ctx", "kvh", None),
        P("exp", "kvh", "ctx"),
        P("exp", "kvh", None),
        P("exp", "kvh", None),
        P("kvh", "ctx", None, None),
        P("exp", None),
        P(),
        P("exp", None),
        P("exp", None),
        P(("ctx", "exp"), None, None, "kvh"),
        P(("ctx", "exp"), "kvh", None),
    )
    out_specs = P("exp", ("ctx", "kvh"))
    return jax.shard_map(body, mesh=mesh, in_specs=in_specs, out_specs=out_specs, check_vma=False)
```

```python
import functools
import math

import jax
import jax.numpy as jnp
from jax import lax
from jax.experimental import pallas as pl
from jax.experimental.pallas import tpu as pltpu
from jax.sharding import PartitionSpec as P

VMEM_SPEC = pl.BlockSpec(memory_space=pltpu.VMEM)
SMEM_SPEC = pl.BlockSpec(memory_space=pltpu.SMEM)
ANY_SPEC = pl.BlockSpec(memory_space=pl.ANY)
MASKED = -1e30
ROW_SLOTS = 2


def in_hbm(value):
    return pltpu.with_memory_space_constraint(value, pltpu.HBM)


def attention_kernel(
    selected_in,
    queries_in,
    new_key_in,
    new_value_in,
    centroid_keys,
    centroid_values,
    key_cache,
    value_cache,
    weight_in,
    out,
    weight_out,
    selected,
    queries,
    new_key,
    new_value,
    keys,
    values,
    small_sem,
    picked_sem,
):
    seq_count, heads_kv, query_count, head_dim = queries.shape
    centroid_rows = centroid_keys.shape[1]
    clusters = centroid_rows // heads_kv
    sel_count = selected.shape[1]
    block_rows = key_cache.shape[1] // clusters
    ctx_pos = lax.axis_index("ctx")
    pairs = (
        (selected_in, selected),
        (centroid_keys, keys.at[:, pl.ds(0, centroid_rows)]),
        (queries_in, queries),
        (new_key_in, new_key),
        (new_value_in, new_value),
        (centroid_values, values.at[:, pl.ds(0, centroid_rows)]),
        (weight_in, weight_out),
    )
    small = [
        pltpu.make_async_copy(source, held, small_sem.at[i]) for i, (source, held) in enumerate(pairs)
    ]
    for copy in small[:6]:
        copy.start()
    small[0].wait()
    picked = ([], [])
    for which, (source, held) in enumerate(((key_cache, keys), (value_cache, values))):
        for s in range(seq_count):
            for g in range(heads_kv):
                for j in range(sel_count):
                    block = selected[g, j, s] - ctx_pos * clusters
                    start = pl.multiple_of(block * block_rows, block_rows)
                    place = centroid_rows + (g * sel_count + j) * block_rows
                    copy = pltpu.make_async_copy(
                        source.at[s, pl.ds(start, block_rows)],
                        held.at[s, pl.ds(place, block_rows)],
                        picked_sem.at[which, s, g * sel_count + j],
                    )
                    copy.start()
                    picked[which].append(copy)
    small[6].start()
    for copy in small[1:4] + picked[0]:
        copy.wait()
    rows = keys.shape[1]
    heads = heads_kv * query_count
    shape = (seq_count * heads, rows)
    head_of_query = lax.broadcasted_iota(jnp.int32, shape, 0) // query_count % heads_kv
    column = lax.broadcasted_iota(jnp.int32, shape, 1)
    head_of_block = (column - centroid_rows) // (sel_count * block_rows)
    valid = (column % heads_kv == head_of_query) & (
        (column < centroid_rows) | (head_of_block == head_of_query)
    )
    score_scale = 1.0 / math.sqrt(head_dim)
    scores, own = [], []
    for s in range(seq_count):
        scores.append(
            lax.dot_general(
                queries[s].reshape(heads, head_dim),
                keys[s],
                (((1,), (1,)), ((), ())),
                preferred_element_type=jnp.float32,
            )
        )
        products = queries[s].astype(jnp.float32) * new_key[s].astype(jnp.float32)[:, None, :]
        own.append(jnp.sum(products, axis=-1, keepdims=True).reshape(heads, 1))
    scores = jnp.where(valid, jnp.concatenate(scores, axis=0) * score_scale, MASKED)
    own = jnp.where(ctx_pos == 0, jnp.concatenate(own, axis=0) * score_scale, MASKED)
    peak = jnp.maximum(jnp.max(scores, axis=-1, keepdims=True), own)
    probs = jnp.exp(scores - peak)
    own_prob = jnp.exp(own - peak)
    total = jnp.sum(probs, axis=-1, keepdims=True) + own_prob
    probs = probs.astype(jnp.bfloat16)
    lane = lax.broadcasted_iota(jnp.int32, (seq_count * heads, head_dim), 1)
    stats = jnp.where(lane < head_dim // 2, peak, total)
    for copy in small[4:6] + picked[1]:
        copy.wait()
    for s in range(seq_count):
        mine = slice(s * heads, (s + 1) * heads)
        weighted = jnp.dot(probs[mine], values[s], preferred_element_type=jnp.float32)
        own_value = jnp.broadcast_to(
            new_value[s].astype(jnp.float32)[:, None, :], (heads_kv, query_count, head_dim)
        ).reshape(heads, head_dim)
        weighted = weighted + own_prob[mine] * own_value
        for g in range(heads_kv):
            part = slice(g * query_count, (g + 1) * query_count)
            out[:, g * seq_count + s, :] = weighted[part]
            out[:, (heads_kv + g) * seq_count + s, :] = stats[mine][part]
    small[6].wait()


def attention(
    queries, key_cache, value_cache, centroid_keys, centroid_values, selected, new_key, new_value, weight
):
    seq_count, heads_kv, query_count, head_dim = queries.shape
    clusters = centroid_keys.shape[1]
    sel_count = selected.shape[2]
    block_rows = key_cache.shape[1] // clusters * heads_kv
    selected = selected.transpose(1, 2, 0)
    centroid_keys, centroid_values, key_cache, value_cache = (
        value.reshape(seq_count, -1, head_dim)
        for value in (centroid_keys, centroid_values, key_cache, value_cache)
    )
    held_rows = clusters * heads_kv + heads_kv * sel_count * block_rows
    held = pltpu.VMEM((seq_count, held_rows, head_dim), jnp.bfloat16)
    operands = (
        selected, queries, new_key, new_value, centroid_keys, centroid_values, key_cache, value_cache, weight
    )
    return pl.pallas_call(
        attention_kernel,
        out_shape=(
            pltpu.VMEM((query_count, 2 * heads_kv * seq_count, head_dim), jnp.float32),
            pltpu.VMEM(weight.shape, weight.dtype),
        ),
        in_specs=[ANY_SPEC] * 9,
        out_specs=(VMEM_SPEC, VMEM_SPEC),
        scratch_shapes=[
            pltpu.SMEM(selected.shape, selected.dtype),
            pltpu.VMEM(queries.shape, queries.dtype),
            pltpu.VMEM(new_key.shape, new_key.dtype),
            pltpu.VMEM(new_value.shape, new_value.dtype),
            held,
            held,
            pltpu.SemaphoreType.DMA((7,)),
            pltpu.SemaphoreType.DMA((2, seq_count, heads_kv * sel_count)),
        ],
        compiler_params=pltpu.CompilerParams(vmem_limit_bytes=12 << 20),
    )(*[in_hbm(operand) for operand in operands])


def project_kernel(parts, weight, out):
    rows = parts.shape[1] // 2
    half = parts.shape[2] // 2
    weighted = parts[:, :rows, :]
    peak = parts[:, rows:, 0:1]
    total = parts[:, rows:, half : half + 1]
    scale = jnp.exp(peak - jnp.max(peak, axis=0, keepdims=True))
    total = jnp.sum(total * scale, axis=0)
    attended = (jnp.sum(weighted * scale, axis=0) / total).astype(jnp.bfloat16)
    seq_count = out.shape[0]
    sums = None
    for g in range(weight.shape[0]):
        term = jnp.dot(
            attended[g * seq_count : (g + 1) * seq_count],
            weight[g, 0],
            preferred_element_type=jnp.float32,
        )
        sums = term if sums is None else sums + term
    out[...] = sums.astype(jnp.bfloat16)


def project(parts, weight):
    seq_count = parts.shape[1] // (2 * weight.shape[0])
    return pl.pallas_call(
        project_kernel,
        out_shape=jax.ShapeDtypeStruct((seq_count, weight.shape[3]), jnp.bfloat16),
        in_specs=[VMEM_SPEC, VMEM_SPEC],
        out_specs=VMEM_SPEC,
        compiler_params=pltpu.CompilerParams(vmem_limit_bytes=8 << 20),
    )(parts, weight)


def fetch_kernel(first, source, *refs):
    out, sem = refs[-2:]
    count = out.shape[0]
    chunks = 4
    part = source.shape[1] // chunks
    copies = [
        pltpu.make_async_copy(
            source.at[0, pl.ds(c * part, part), :, pl.ds((first + t) * 128, 128)],
            out.at[t, pl.ds(c * part, part)],
            sem.at[t, c],
        )
        for c in range(chunks)
        for t in range(count)
    ]
    for copy in copies:
        copy.start()
    for copy in copies:
        copy.wait()


def fetch(weights, first, count, *after):
    depth = weights.shape[1]
    tiles = pl.pallas_call(
        functools.partial(fetch_kernel, first),
        out_shape=pltpu.VMEM((count, depth, 2, 128), weights.dtype),
        in_specs=[ANY_SPEC] * (1 + len(after)),
        out_specs=VMEM_SPEC,
        scratch_shapes=[pltpu.SemaphoreType.DMA((count, 4))],
        compiler_params=pltpu.CompilerParams(vmem_limit_bytes=1 << 20),
        cost_estimate=pl.CostEstimate(
            flops=0, bytes_accessed=count * depth * 512, transcendentals=0
        ),
    )(in_hbm(weights), *after)
    return tiles.reshape(count, 2 * depth, 128)


def experts_kernel(order, x0, x1, *refs):
    *tiles, down, out, spread = refs
    half = x0.shape[0]
    model_dim = spread.shape[1] // 2
    rows = 2 * half
    blocks = len(order)
    seq_count = rows // blocks
    slots = out.shape[1] // 2
    exp_pos = lax.axis_index("exp")
    names = jnp.concatenate([x0[:, model_dim:], x1[:, model_dim:]], axis=0).astype(jnp.float32)
    lane = lax.broadcasted_iota(jnp.int32, names.shape, 1)
    here = lax.axis_index("ctx") * blocks + exp_pos
    named = jnp.sum(jnp.where(lane == here, names, 0.0), axis=-1, keepdims=True)
    row = lax.broadcasted_iota(jnp.int32, (rows, rows), 0)
    col = lax.broadcasted_iota(jnp.int32, (rows, rows), 1)
    earlier = (row // seq_count == col // seq_count) & (row < col)
    ones = jnp.ones((blocks * slots, rows), jnp.bfloat16)
    by_column = jnp.dot(
        ones, jnp.where(row == col, named, 0.0).astype(jnp.bfloat16), preferred_element_type=jnp.float32
    )
    rank = jnp.dot(
        ones, jnp.where(earlier, named, 0.0).astype(jnp.bfloat16), preferred_element_type=jnp.float32
    )
    slot = lax.broadcasted_iota(jnp.int32, by_column.shape, 0)
    member = lax.broadcasted_iota(jnp.int32, by_column.shape, 1)
    chosen = (by_column > 0.5) & (slot // slots == member // seq_count)
    chosen = chosen & (jnp.abs(rank - (slot % slots).astype(jnp.float32)) < 0.5)
    chosen = jnp.where(chosen, 1.0, 0.0).astype(jnp.bfloat16)
    source = lax.broadcasted_iota(jnp.int32, (128, 512), 0)
    target = lax.broadcasted_iota(jnp.int32, (128, 512), 1)
    ends = (target == 2 * source) | (target == 2 * source + 257)
    to_both = jnp.where(ends, 1.0, 0.0).astype(jnp.bfloat16)
    pieces = []
    for j in range(model_dim // 128):
        pieces += [x[:, j * 128 : (j + 1) * 128] for x in (x0, x1)]
    result = jnp.dot(
        jnp.concatenate(pieces, axis=0), to_both, preferred_element_type=jnp.float32
    ).astype(jnp.bfloat16)
    for j in range(model_dim // 128):
        columns = slice(j * 256, (j + 1) * 256)
        spread[0:rows, columns] = result[j * rows : (j + 1) * rows, 0:256]
        spread[rows : 2 * rows, columns] = result[j * rows : (j + 1) * rows, 256:512]
    lanes = [tile.at[t] for tile in tiles for t in range(tile.shape[0])]
    depth = 1024
    both = []
    for u in range(len(lanes) // 2):
        total = jnp.zeros((2 * rows, 256), jnp.float32)
        for c in range(2 * model_dim // depth):
            here = slice(c * depth, (c + 1) * depth)
            right = jnp.concatenate([lanes[2 * u][here, :], lanes[2 * u + 1][here, :]], axis=1)
            total = total + jnp.dot(spread[:, here], right, preferred_element_type=jnp.float32)
        both.append(total)
    both = jnp.concatenate(both, axis=1)
    gate, up = both[:rows], both[rows:]
    activated = (jax.nn.silu(gate) * up).astype(jnp.bfloat16)
    activated = jnp.dot(chosen, activated, preferred_element_type=jnp.float32).astype(jnp.bfloat16)
    width = 1024

    def down_part(b, carry):
        columns = pl.ds(pl.multiple_of(b * width, width), width)
        result = jnp.dot(
            activated, down[0, :, columns], preferred_element_type=jnp.float32
        ).astype(jnp.bfloat16)
        for q in range(width // 256):
            for p, i in enumerate(order):
                place = (b * (width // 256) + q) * blocks + lax.bitwise_xor(exp_pos, i)
                mine = result[p * slots : (p + 1) * slots]
                out[place, 0:slots] = mine[:, q * 256 : q * 256 + 128]
                out[place, slots : 2 * slots] = mine[:, q * 256 + 128 : (q + 1) * 256]
        return carry

    lax.fori_loop(0, model_dim // width, down_part, 0)


def experts(pieces, tiles, down, order, slots):
    half = pieces[0].shape[0]
    model_dim = down.shape[2]
    rows = 2 * half
    blocks = len(order)
    return pl.pallas_call(
        functools.partial(experts_kernel, order),
        out_shape=pltpu.VMEM((model_dim // 256 * blocks, 2 * slots, 128), jnp.bfloat16),
        in_specs=[VMEM_SPEC] * (3 + len(tiles)),
        out_specs=VMEM_SPEC,
        scratch_shapes=[pltpu.VMEM((2 * rows, 2 * model_dim), jnp.bfloat16)],
        compiler_params=pltpu.CompilerParams(vmem_limit_bytes=16 << 20),
    )(*pieces, *tiles, down)


def sum_kernel(p0, p1, p2, p3, before, out):
    total = p0[...].astype(jnp.float32)
    for piece in (p1, p2, p3):
        total = total + piece[...].astype(jnp.float32)
    out[...] = total.astype(out.dtype)


def sum_pieces(pieces, before):
    return pl.pallas_call(
        sum_kernel,
        out_shape=pltpu.VMEM(pieces[0].shape, pieces[0].dtype),
        in_specs=[VMEM_SPEC] * 4 + [ANY_SPEC],
        out_specs=VMEM_SPEC,
        compiler_params=pltpu.CompilerParams(vmem_limit_bytes=2 << 20),
    )(*pieces, before)


def norm_kernel(kvh_devices, p0, p1, p2, p3, residual, gain, ids, before, own, normed):
    total = residual[...].astype(jnp.float32)
    for piece in (p0, p1, p2, p3):
        total = total + piece[...].astype(jnp.float32)
    seq_count, model_dim = total.shape
    mean_square = jnp.mean(total * total, axis=-1, keepdims=True)
    rows = total * lax.rsqrt(mean_square + 1e-06) * gain[...]
    normed[:, :model_dim] = rows.astype(normed.dtype)
    lane = lax.broadcasted_iota(jnp.int32, (seq_count, normed.shape[1] - model_dim), 1)
    names = jnp.zeros(lane.shape, jnp.float32)
    for k in range(ids.shape[1]):
        names = jnp.where(ids[:, k : k + 1] == lane, 1.0, names)
    normed[:, model_dim:] = names.astype(normed.dtype)
    place = lax.axis_index("ctx") * kvh_devices + lax.axis_index("kvh")
    width = own.shape[1]
    for p in range(model_dim // width):
        @pl.when(place == p)
        def _():
            own[...] = total[:, p * width : (p + 1) * width]


def norm(pieces, residual, gain, ids, before, kvh_devices):
    seq_count, model_dim = residual.shape
    return pl.pallas_call(
        functools.partial(norm_kernel, kvh_devices),
        out_shape=(
            pltpu.VMEM((seq_count, 256), jnp.float32),
            pltpu.VMEM((seq_count, model_dim + 128), jnp.bfloat16),
        ),
        in_specs=[VMEM_SPEC] * 7 + [ANY_SPEC],
        out_specs=(VMEM_SPEC,) * 2,
        compiler_params=pltpu.CompilerParams(vmem_limit_bytes=2 << 20),
    )(*pieces, residual, gain.reshape(1, -1), ids, before)


def weights_kernel(sizes, ids, gates, after, mix):
    kvh_devices, exp_devices, slots = sizes
    seq_count = ids.shape[0]
    shape = (seq_count, mix.shape[1])
    column = lax.broadcasted_iota(jnp.int32, shape, 1)
    device = column // (2 * slots)
    expert = device // (kvh_devices * exp_devices) * exp_devices + device % exp_devices
    weight = jnp.zeros(shape, jnp.float32)
    named = jnp.zeros(shape, jnp.float32)
    for k in range(ids.shape[1]):
        match = ids[:, k : k + 1] == expert
        weight = jnp.where(match, gates[:, k : k + 1], weight)
        named = jnp.where(match, 1.0, named)
    rank = [jnp.zeros((1, shape[1]), jnp.float32)]
    for r in range(seq_count - 1):
        rank.append(rank[-1] + named[r : r + 1])
    rank = jnp.concatenate(rank, axis=0)
    slot = (column % slots).astype(jnp.float32)
    weight = jnp.where(jnp.abs(rank - slot) < 0.5, weight, 0.0)
    half = column // slots % 2
    weight = jnp.concatenate([jnp.where(half == h, weight, 0.0) for h in range(2)], axis=0)
    high = weight.astype(jnp.bfloat16)
    mix[0 : 2 * seq_count] = high
    mix[2 * seq_count : 4 * seq_count] = (weight - high.astype(jnp.float32)).astype(jnp.bfloat16)


def mixing_weights(ids, gates, after, sizes, devices):
    slots = sizes[2]
    return pl.pallas_call(
        functools.partial(weights_kernel, sizes),
        out_shape=pltpu.VMEM((4 * ids.shape[0], devices * 2 * slots), jnp.bfloat16),
        in_specs=[VMEM_SPEC] * 2 + [ANY_SPEC],
        out_specs=VMEM_SPEC,
        compiler_params=pltpu.CompilerParams(vmem_limit_bytes=2 << 20),
    )(ids, gates, after)


def stack_kernel(p0, p1, p2, p3, before, out):
    out[...] = jnp.concatenate([p0[...], p1[...], p2[...], p3[...]], axis=0)


def stack(pieces, before):
    rows, columns = pieces[0].shape
    return pl.pallas_call(
        stack_kernel,
        out_shape=pltpu.VMEM((4 * rows, columns), pieces[0].dtype),
        in_specs=[VMEM_SPEC] * 4 + [ANY_SPEC],
        out_specs=VMEM_SPEC,
        compiler_params=pltpu.CompilerParams(vmem_limit_bytes=2 << 20),
    )(*pieces, before)


def mix_kernel(returned, mix, own, out):
    seq_count = own.shape[0]
    sums = jnp.dot(mix[...], returned[...], preferred_element_type=jnp.float32)
    sums = sums[0 : 2 * seq_count] + sums[2 * seq_count : 4 * seq_count]
    width = sums.shape[1]
    out[:, 0:width] = (own[:, 0:width] + sums[0:seq_count]).astype(out.dtype)
    out[:, width : 2 * width] = (own[:, width : 2 * width] + sums[seq_count:]).astype(out.dtype)


def mix_results(returned, mix, own):
    return pl.pallas_call(
        mix_kernel,
        out_shape=jax.ShapeDtypeStruct(own.shape, jnp.bfloat16),
        in_specs=[VMEM_SPEC] * 3,
        out_specs=VMEM_SPEC,
        compiler_params=pltpu.CompilerParams(vmem_limit_bytes=2 << 20),
    )(returned.reshape(-1, returned.shape[2]), mix, own)


def swapped(value, axes, count, mask):
    return lax.ppermute(value, axes, [(i, i ^ mask) for i in range(count)])


def body(
    queries,
    key_cache,
    value_cache,
    centroid_keys,
    centroid_values,
    selected,
    new_key,
    new_value,
    out_weight,
    residual,
    norm_gain,
    expert_ids,
    gate_weights,
    w_gate_up,
    w_down,
):
    ctx_devices = lax.axis_size("ctx")
    kvh_devices = lax.axis_size("kvh")
    exp_devices = lax.axis_size("exp")
    plane = ctx_devices * kvh_devices

    parts, out_weight = attention(
        queries,
        key_cache,
        value_cache,
        centroid_keys,
        centroid_values,
        selected,
        new_key,
        new_value,
        out_weight,
    )
    parts = lax.all_to_all(parts, "ctx", split_axis=0, concat_axis=0, tiled=True)

    projected = project(parts, out_weight)

    axes = ("ctx", "kvh")
    along_x = [projected] + [swapped(projected, axes, plane, m) for m in (1, 2, 3)]
    tiles = [fetch(w_gate_up, 0, 2, projected)]
    sums = sum_pieces(along_x, tiles[0])
    along_z = [sums] + [swapped(sums, axes, plane, m) for m in range(4, plane, 4)]
    tiles.append(fetch(w_gate_up, 2, 2, sums))
    own, normed = norm(along_z, residual, norm_gain, expert_ids, tiles[1], kvh_devices)

    steps = range(0, exp_devices, 2)
    along_y = [normed] + [swapped(normed, "exp", exp_devices, m) for m in steps[1:]]
    tiles.append(fetch(w_gate_up, 4, 2, normed))
    mine = stack(along_y, tiles[2])
    other = swapped(mine, "exp", exp_devices, 1)
    order = tuple(steps) + tuple(m + 1 for m in steps)
    results = experts((mine, other), tiles, w_down, order, ROW_SLOTS)
    returned = lax.all_to_all(
        results, ("ctx", "kvh", "exp"), split_axis=0, concat_axis=0, tiled=True
    )
    sizes = (kvh_devices, exp_devices, ROW_SLOTS)
    mix = mixing_weights(expert_ids, gate_weights, results, sizes, plane * exp_devices)
    return mix_results(returned, mix, own)


def solution(mesh):
    in_specs = (
        P("exp", "kvh", None, None),
        P("exp", "ctx", "kvh", None),
        P("exp", "ctx", "kvh", None),
        P("exp", "ctx", "kvh", None),
        P("exp", "ctx", "kvh", None),
        P("exp", "kvh", "ctx"),
        P("exp", "kvh", None),
        P("exp", "kvh", None),
        P("kvh", "ctx", None, None),
        P("exp", None),
        P(),
        P("exp", None),
        P("exp", None),
        P(("ctx", "exp"), None, None, "kvh"),
        P(("ctx", "exp"), "kvh", None),
    )
    out_specs = P("exp", ("ctx", "kvh"))
    return jax.shard_map(body, mesh=mesh, in_specs=in_specs, out_specs=out_specs, check_vma=False)
```

```python
import functools
import math

import jax
import jax.numpy as jnp
from jax import lax
from jax.experimental import pallas as pl
from jax.experimental.pallas import tpu as pltpu
from jax.sharding import PartitionSpec as P

VMEM_SPEC = pl.BlockSpec(memory_space=pltpu.VMEM)
SMEM_SPEC = pl.BlockSpec(memory_space=pltpu.SMEM)
ANY_SPEC = pl.BlockSpec(memory_space=pl.ANY)
MASKED = -1e30
ROW_SLOTS = 2


def in_hbm(value):
    return pltpu.with_memory_space_constraint(value, pltpu.HBM)


def tile_copies(source, first, out, sem):
    chunks = sem.shape[1]
    part = source.shape[1] // chunks
    return [
        pltpu.make_async_copy(
            source.at[0, pl.ds(c * part, part), :, pl.ds((first + t) * 128, 128)],
            out.at[t, pl.ds(c * part, part)],
            sem.at[t, c],
        )
        for c in range(chunks)
        for t in range(out.shape[0])
    ]


def attention_kernel(
    selected_in,
    queries_in,
    new_key_in,
    new_value_in,
    centroid_keys,
    centroid_values,
    key_cache,
    value_cache,
    weight_in,
    out,
    weight_out,
    selected,
    queries,
    new_key,
    new_value,
    keys,
    values,
    small_sem,
    picked_sem,
):
    seq_count, heads_kv, query_count, head_dim = queries.shape
    centroid_rows = centroid_keys.shape[1]
    clusters = centroid_rows // heads_kv
    sel_count = selected.shape[1]
    block_rows = key_cache.shape[1] // clusters
    ctx_pos = lax.axis_index("ctx")
    pairs = (
        (selected_in, selected),
        (centroid_keys, keys.at[:, pl.ds(0, centroid_rows)]),
        (queries_in, queries),
        (new_key_in, new_key),
        (new_value_in, new_value),
        (centroid_values, values.at[:, pl.ds(0, centroid_rows)]),
        (weight_in, weight_out),
    )
    small = [
        pltpu.make_async_copy(source, held, small_sem.at[i]) for i, (source, held) in enumerate(pairs)
    ]
    for copy in small:
        copy.start()
    small[0].wait()
    picked = ([], [])
    for which, (source, held) in enumerate(((key_cache, keys), (value_cache, values))):
        for s in range(seq_count):
            for g in range(heads_kv):
                for j in range(sel_count):
                    block = selected[g, j, s] - ctx_pos * clusters
                    start = pl.multiple_of(block * block_rows, block_rows)
                    place = centroid_rows + (g * sel_count + j) * block_rows
                    copy = pltpu.make_async_copy(
                        source.at[s, pl.ds(start, block_rows)],
                        held.at[s, pl.ds(place, block_rows)],
                        picked_sem.at[which, s, g * sel_count + j],
                    )
                    copy.start()
                    picked[which].append(copy)
    for copy in small[1:4] + picked[0]:
        copy.wait()
    rows = keys.shape[1]
    heads = heads_kv * query_count
    shape = (seq_count * heads, rows)
    head_of_query = lax.broadcasted_iota(jnp.int32, shape, 0) // query_count % heads_kv
    column = lax.broadcasted_iota(jnp.int32, shape, 1)
    head_of_block = (column - centroid_rows) // (sel_count * block_rows)
    valid = (column % heads_kv == head_of_query) & (
        (column < centroid_rows) | (head_of_block == head_of_query)
    )
    score_scale = 1.0 / math.sqrt(head_dim)
    scores, own = [], []
    for s in range(seq_count):
        scores.append(
            lax.dot_general(
                queries[s].reshape(heads, head_dim),
                keys[s],
                (((1,), (1,)), ((), ())),
                preferred_element_type=jnp.float32,
            )
        )
        products = queries[s].astype(jnp.float32) * new_key[s].astype(jnp.float32)[:, None, :]
        own.append(jnp.sum(products, axis=-1, keepdims=True).reshape(heads, 1))
    scores = jnp.where(valid, jnp.concatenate(scores, axis=0) * score_scale, MASKED)
    own = jnp.where(ctx_pos == 0, jnp.concatenate(own, axis=0) * score_scale, MASKED)
    peak = jnp.maximum(jnp.max(scores, axis=-1, keepdims=True), own)
    probs = jnp.exp(scores - peak)
    own_prob = jnp.exp(own - peak)
    total = jnp.sum(probs, axis=-1, keepdims=True) + own_prob
    probs = probs.astype(jnp.bfloat16)
    lane = lax.broadcasted_iota(jnp.int32, (seq_count * heads, head_dim), 1)
    stats = jnp.where(lane < head_dim // 2, peak, total)
    for copy in small[4:6] + picked[1]:
        copy.wait()
    for s in range(seq_count):
        mine = slice(s * heads, (s + 1) * heads)
        weighted = jnp.dot(probs[mine], values[s], preferred_element_type=jnp.float32)
        own_value = jnp.broadcast_to(
            new_value[s].astype(jnp.float32)[:, None, :], (heads_kv, query_count, head_dim)
        ).reshape(heads, head_dim)
        weighted = weighted + own_prob[mine] * own_value
        for g in range(heads_kv):
            part = slice(g * query_count, (g + 1) * query_count)
            out[:, g * seq_count + s, :] = weighted[part]
            out[:, (heads_kv + g) * seq_count + s, :] = stats[mine][part]
    small[6].wait()


def attention(
    queries, key_cache, value_cache, centroid_keys, centroid_values, selected, new_key, new_value, weight
):
    seq_count, heads_kv, query_count, head_dim = queries.shape
    clusters = centroid_keys.shape[1]
    sel_count = selected.shape[2]
    block_rows = key_cache.shape[1] // clusters * heads_kv
    selected = selected.transpose(1, 2, 0)
    centroid_keys, centroid_values, key_cache, value_cache = (
        value.reshape(seq_count, -1, head_dim)
        for value in (centroid_keys, centroid_values, key_cache, value_cache)
    )
    held_rows = clusters * heads_kv + heads_kv * sel_count * block_rows
    held = pltpu.VMEM((seq_count, held_rows, head_dim), jnp.bfloat16)
    operands = (
        selected, queries, new_key, new_value, centroid_keys, centroid_values, key_cache, value_cache, weight
    )
    return pl.pallas_call(
        attention_kernel,
        out_shape=(
            pltpu.VMEM((query_count, 2 * heads_kv * seq_count, head_dim), jnp.float32),
            pltpu.VMEM(weight.shape, weight.dtype),
        ),
        in_specs=[ANY_SPEC] * 9,
        out_specs=(VMEM_SPEC, VMEM_SPEC),
        scratch_shapes=[
            pltpu.SMEM(selected.shape, selected.dtype),
            pltpu.VMEM(queries.shape, queries.dtype),
            pltpu.VMEM(new_key.shape, new_key.dtype),
            pltpu.VMEM(new_value.shape, new_value.dtype),
            held,
            held,
            pltpu.SemaphoreType.DMA((7,)),
            pltpu.SemaphoreType.DMA((2, seq_count, heads_kv * sel_count)),
        ],
        compiler_params=pltpu.CompilerParams(vmem_limit_bytes=12 << 20),
    )(*[in_hbm(operand) for operand in operands])


def project_kernel(parts, weight, out):
    rows = parts.shape[1] // 2
    half = parts.shape[2] // 2
    weighted = parts[:, :rows, :]
    peak = parts[:, rows:, 0:1]
    total = parts[:, rows:, half : half + 1]
    scale = jnp.exp(peak - jnp.max(peak, axis=0, keepdims=True))
    total = jnp.sum(total * scale, axis=0)
    attended = (jnp.sum(weighted * scale, axis=0) / total).astype(jnp.bfloat16)
    seq_count = out.shape[0]
    sums = None
    for g in range(weight.shape[0]):
        term = jnp.dot(
            attended[g * seq_count : (g + 1) * seq_count],
            weight[g, 0],
            preferred_element_type=jnp.float32,
        )
        sums = term if sums is None else sums + term
    out[...] = sums.astype(jnp.bfloat16)


def project(parts, weight):
    seq_count = parts.shape[1] // (2 * weight.shape[0])
    return pl.pallas_call(
        project_kernel,
        out_shape=jax.ShapeDtypeStruct((seq_count, weight.shape[3]), jnp.bfloat16),
        in_specs=[VMEM_SPEC, VMEM_SPEC],
        out_specs=VMEM_SPEC,
        compiler_params=pltpu.CompilerParams(vmem_limit_bytes=8 << 20),
    )(parts, weight)


def fetch_kernel(first, source, *refs):
    out, sem = refs[-2:]
    copies = tile_copies(source, first, out, sem)
    for copy in copies:
        copy.start()
    for copy in copies:
        copy.wait()


def fetch(weights, first, count, *after):
    depth = weights.shape[1]
    tiles = pl.pallas_call(
        functools.partial(fetch_kernel, first),
        out_shape=pltpu.VMEM((count, depth, 2, 128), weights.dtype),
        in_specs=[ANY_SPEC] * (1 + len(after)),
        out_specs=VMEM_SPEC,
        scratch_shapes=[pltpu.SemaphoreType.DMA((count, 4))],
        compiler_params=pltpu.CompilerParams(vmem_limit_bytes=1 << 20),
        cost_estimate=pl.CostEstimate(
            flops=0, bytes_accessed=count * depth * 512, transcendentals=0
        ),
    )(in_hbm(weights), *after)
    return tiles.reshape(count, 2 * depth, 128)


def spread_rows(x, model_dim, spread):
    rows = x.shape[0]
    source = lax.broadcasted_iota(jnp.int32, (128, 512), 0)
    target = lax.broadcasted_iota(jnp.int32, (128, 512), 1)
    ends = (target == 2 * source) | (target == 2 * source + 257)
    to_both = jnp.where(ends, 1.0, 0.0).astype(jnp.bfloat16)
    pieces = [x[:, j * 128 : (j + 1) * 128] for j in range(model_dim // 128)]
    result = jnp.dot(
        jnp.concatenate(pieces, axis=0), to_both, preferred_element_type=jnp.float32
    ).astype(jnp.bfloat16)
    for j in range(model_dim // 128):
        columns = slice(j * 256, (j + 1) * 256)
        spread[0:rows, columns] = result[j * rows : (j + 1) * rows, 0:256]
        spread[rows : 2 * rows, columns] = result[j * rows : (j + 1) * rows, 256:512]


def spread_kernel(x, spread):
    spread_rows(x, spread.shape[1] // 2, spread)


def spread_alone(x, model_dim):
    return pl.pallas_call(
        spread_kernel,
        out_shape=pltpu.VMEM((2 * x.shape[0], 2 * model_dim), x.dtype),
        in_specs=[VMEM_SPEC],
        out_specs=VMEM_SPEC,
        compiler_params=pltpu.CompilerParams(vmem_limit_bytes=4 << 20),
        cost_estimate=pl.CostEstimate(flops=0, bytes_accessed=1 << 20, transcendentals=0),
    )(x)


def experts_kernel(order, x0, x1, first, *refs):
    *tiles, down, out, second = refs
    half = x0.shape[0]
    model_dim = second.shape[1] // 2
    rows = 2 * half
    blocks = len(order)
    seq_count = rows // blocks
    slots = out.shape[1] // 2
    exp_pos = lax.axis_index("exp")
    names = jnp.concatenate([x0[:, model_dim:], x1[:, model_dim:]], axis=0).astype(jnp.float32)
    lane = lax.broadcasted_iota(jnp.int32, names.shape, 1)
    here = lax.axis_index("ctx") * blocks + exp_pos
    code = jnp.sum(jnp.where(lane == here, names, 0.0), axis=-1, keepdims=True)
    row = lax.broadcasted_iota(jnp.int32, names.shape, 0)
    place = row // seq_count * slots + code.astype(jnp.int32) - 1
    chosen = jnp.where((code > 0.5) & (place == lane), 1.0, 0.0)
    chosen = chosen.T[: blocks * slots].astype(jnp.bfloat16)
    spread_rows(x1, model_dim, second)
    lanes = [tile.at[t] for tile in tiles for t in range(tile.shape[0])]
    depth = 1024
    both = []
    for u in range(len(lanes) // 2):
        total = jnp.zeros((2 * rows, 256), jnp.float32)
        for c in range(2 * model_dim // depth):
            here = slice(c * depth, (c + 1) * depth)
            right = jnp.concatenate([lanes[2 * u][here, :], lanes[2 * u + 1][here, :]], axis=1)
            left = jnp.concatenate([first[:, here], second[:, here]], axis=0)
            total = total + jnp.dot(left, right, preferred_element_type=jnp.float32)
        both.append(total)
    both = jnp.concatenate(both, axis=1)
    gate = jnp.concatenate([both[0:half], both[rows : rows + half]], axis=0)
    up = jnp.concatenate([both[half:rows], both[rows + half :]], axis=0)
    activated = (jax.nn.silu(gate) * up).astype(jnp.bfloat16)
    activated = jnp.dot(chosen, activated, preferred_element_type=jnp.float32).astype(jnp.bfloat16)
    width = 2048

    def down_part(b, carry):
        columns = pl.ds(pl.multiple_of(b * width, width), width)
        result = jnp.dot(
            activated, down[0, :, columns], preferred_element_type=jnp.float32
        ).astype(jnp.bfloat16)
        for q in range(width // 256):
            for p, i in enumerate(order):
                place = (b * (width // 256) + q) * blocks + lax.bitwise_xor(exp_pos, i)
                mine = result[p * slots : (p + 1) * slots]
                out[place, 0:slots] = mine[:, q * 256 : q * 256 + 128]
                out[place, slots : 2 * slots] = mine[:, q * 256 + 128 : (q + 1) * 256]
        return carry

    lax.fori_loop(0, model_dim // width, down_part, 0)


def experts(pieces, tiles, down, order, slots):
    half = pieces[0].shape[0]
    model_dim = down.shape[2]
    rows = 2 * half
    blocks = len(order)
    return pl.pallas_call(
        functools.partial(experts_kernel, order),
        out_shape=pltpu.VMEM((model_dim // 256 * blocks, 2 * slots, 128), jnp.bfloat16),
        in_specs=[VMEM_SPEC] * (4 + len(tiles)),
        out_specs=VMEM_SPEC,
        scratch_shapes=[pltpu.VMEM((rows, 2 * model_dim), jnp.bfloat16)],
        compiler_params=pltpu.CompilerParams(vmem_limit_bytes=16 << 20),
    )(*pieces, spread_alone(pieces[0], model_dim), *tiles, down)


def sum_kernel(p0, p1, p2, p3, before, out):
    total = p0[...].astype(jnp.float32)
    for piece in (p1, p2, p3):
        total = total + piece[...].astype(jnp.float32)
    out[...] = total.astype(out.dtype)


def sum_pieces(pieces, before):
    return pl.pallas_call(
        sum_kernel,
        out_shape=pltpu.VMEM(pieces[0].shape, pieces[0].dtype),
        in_specs=[VMEM_SPEC] * 4 + [ANY_SPEC],
        out_specs=VMEM_SPEC,
        compiler_params=pltpu.CompilerParams(vmem_limit_bytes=2 << 20),
    )(*pieces, before)


def norm_kernel(kvh_devices, p0, p1, p2, p3, residual, gain, ids, before, own, normed):
    total = residual[...].astype(jnp.float32)
    for piece in (p0, p1, p2, p3):
        total = total + piece[...].astype(jnp.float32)
    seq_count, model_dim = total.shape
    mean_square = jnp.mean(total * total, axis=-1, keepdims=True)
    rows = total * lax.rsqrt(mean_square + 1e-06) * gain[...]
    normed[:, :model_dim] = rows.astype(normed.dtype)
    lane = lax.broadcasted_iota(jnp.int32, (seq_count, normed.shape[1] - model_dim), 1)
    names = jnp.zeros(lane.shape, jnp.float32)
    for k in range(ids.shape[1]):
        names = jnp.where(ids[:, k : k + 1] == lane, 1.0, names)
    slot = [names[0:1]]
    for r in range(1, seq_count):
        slot.append(slot[-1] + names[r : r + 1])
    normed[:, model_dim:] = (names * jnp.concatenate(slot, axis=0)).astype(normed.dtype)
    place = lax.axis_index("ctx") * kvh_devices + lax.axis_index("kvh")
    width = own.shape[1]
    for p in range(model_dim // width):
        @pl.when(place == p)
        def _():
            own[...] = total[:, p * width : (p + 1) * width]


def norm(pieces, residual, gain, ids, before, kvh_devices):
    seq_count, model_dim = residual.shape
    return pl.pallas_call(
        functools.partial(norm_kernel, kvh_devices),
        out_shape=(
            pltpu.VMEM((seq_count, 256), jnp.float32),
            pltpu.VMEM((seq_count, model_dim + 128), jnp.bfloat16),
        ),
        in_specs=[VMEM_SPEC] * 7 + [ANY_SPEC],
        out_specs=(VMEM_SPEC,) * 2,
        compiler_params=pltpu.CompilerParams(vmem_limit_bytes=2 << 20),
    )(*pieces, residual, gain.reshape(1, -1), ids, before)


def weights_kernel(sizes, ids, gates, after, mix):
    kvh_devices, exp_devices, slots = sizes
    seq_count = ids.shape[0]
    shape = (seq_count, mix.shape[1])
    column = lax.broadcasted_iota(jnp.int32, shape, 1)
    device = column // (2 * slots)
    expert = device // (kvh_devices * exp_devices) * exp_devices + device % exp_devices
    weight = jnp.zeros(shape, jnp.float32)
    named = jnp.zeros(shape, jnp.float32)
    for k in range(ids.shape[1]):
        match = ids[:, k : k + 1] == expert
        weight = jnp.where(match, gates[:, k : k + 1], weight)
        named = jnp.where(match, 1.0, named)
    rank = [jnp.zeros((1, shape[1]), jnp.float32)]
    for r in range(seq_count - 1):
        rank.append(rank[-1] + named[r : r + 1])
    rank = jnp.concatenate(rank, axis=0)
    slot = (column % slots).astype(jnp.float32)
    weight = jnp.where(jnp.abs(rank - slot) < 0.5, weight, 0.0)
    half = column // slots % 2
    weight = jnp.concatenate([jnp.where(half == h, weight, 0.0) for h in range(2)], axis=0)
    high = weight.astype(jnp.bfloat16)
    mix[0 : 2 * seq_count] = high
    mix[2 * seq_count : 4 * seq_count] = (weight - high.astype(jnp.float32)).astype(jnp.bfloat16)


def mixing_weights(ids, gates, after, sizes, devices):
    slots = sizes[2]
    return pl.pallas_call(
        functools.partial(weights_kernel, sizes),
        out_shape=pltpu.VMEM((4 * ids.shape[0], devices * 2 * slots), jnp.bfloat16),
        in_specs=[VMEM_SPEC] * 2 + [ANY_SPEC],
        out_specs=VMEM_SPEC,
        compiler_params=pltpu.CompilerParams(vmem_limit_bytes=2 << 20),
    )(ids, gates, after)


def stack_kernel(p0, p1, p2, p3, before, out):
    out[...] = jnp.concatenate([p0[...], p1[...], p2[...], p3[...]], axis=0)


def stack(pieces, before):
    rows, columns = pieces[0].shape
    return pl.pallas_call(
        stack_kernel,
        out_shape=pltpu.VMEM((4 * rows, columns), pieces[0].dtype),
        in_specs=[VMEM_SPEC] * 4 + [ANY_SPEC],
        out_specs=VMEM_SPEC,
        compiler_params=pltpu.CompilerParams(vmem_limit_bytes=2 << 20),
    )(*pieces, before)


def mix_kernel(returned, mix, own, out):
    seq_count = own.shape[0]
    sums = jnp.dot(mix[...], returned[...], preferred_element_type=jnp.float32)
    sums = sums[0 : 2 * seq_count] + sums[2 * seq_count : 4 * seq_count]
    width = sums.shape[1]
    out[:, 0:width] = (own[:, 0:width] + sums[0:seq_count]).astype(out.dtype)
    out[:, width : 2 * width] = (own[:, width : 2 * width] + sums[seq_count:]).astype(out.dtype)


def mix_results(returned, mix, own):
    return pl.pallas_call(
        mix_kernel,
        out_shape=jax.ShapeDtypeStruct(own.shape, jnp.bfloat16),
        in_specs=[VMEM_SPEC] * 3,
        out_specs=VMEM_SPEC,
        compiler_params=pltpu.CompilerParams(vmem_limit_bytes=2 << 20),
    )(returned.reshape(-1, returned.shape[2]), mix, own)


def swapped(value, axes, count, mask):
    return lax.ppermute(value, axes, [(i, i ^ mask) for i in range(count)])


def body(
    queries,
    key_cache,
    value_cache,
    centroid_keys,
    centroid_values,
    selected,
    new_key,
    new_value,
    out_weight,
    residual,
    norm_gain,
    expert_ids,
    gate_weights,
    w_gate_up,
    w_down,
):
    ctx_devices = lax.axis_size("ctx")
    kvh_devices = lax.axis_size("kvh")
    exp_devices = lax.axis_size("exp")
    plane = ctx_devices * kvh_devices

    parts, out_weight = attention(
        queries,
        key_cache,
        value_cache,
        centroid_keys,
        centroid_values,
        selected,
        new_key,
        new_value,
        out_weight,
    )
    parts = lax.all_to_all(parts, "ctx", split_axis=0, concat_axis=0, tiled=True)

    projected = project(parts, out_weight)

    axes = ("ctx", "kvh")
    along_x = [projected] + [swapped(projected, axes, plane, m) for m in (2, 3, 1)]
    tiles = [fetch(w_gate_up, 0, 2, projected)]
    sums = sum_pieces(along_x, tiles[-1])
    along_z = [sums] + [swapped(sums, axes, plane, m) for m in (4, 12, 8)]
    tiles.append(fetch(w_gate_up, 2, 2, sums))
    own, normed = norm(along_z, residual, norm_gain, expert_ids, tiles[-1], kvh_devices)

    steps = (0, 2, 6, 4)
    along_y = [normed] + [swapped(normed, "exp", exp_devices, m) for m in steps[1:]]
    tiles.append(fetch(w_gate_up, 4, 2, normed))
    mine = stack(along_y, tiles[-1])
    other = swapped(mine, "exp", exp_devices, 1)
    order = steps + tuple(m + 1 for m in steps)
    results = experts((mine, other), tiles, w_down, order, ROW_SLOTS)
    returned = lax.all_to_all(
        results, ("ctx", "kvh", "exp"), split_axis=0, concat_axis=0, tiled=True
    )
    sizes = (kvh_devices, exp_devices, ROW_SLOTS)
    mix = mixing_weights(expert_ids, gate_weights, results, sizes, plane * exp_devices)
    return mix_results(returned, mix, own)


def solution(mesh):
    in_specs = (
        P("exp", "kvh", None, None),
        P("exp", "ctx", "kvh", None),
        P("exp", "ctx", "kvh", None),
        P("exp", "ctx", "kvh", None),
        P("exp", "ctx", "kvh", None),
        P("exp", "kvh", "ctx"),
        P("exp", "kvh", None),
        P("exp", "kvh", None),
        P("kvh", "ctx", None, None),
        P("exp", None),
        P(),
        P("exp", None),
        P("exp", None),
        P(("ctx", "exp"), None, None, "kvh"),
        P(("ctx", "exp"), "kvh", None),
    )
    out_specs = P("exp", ("ctx", "kvh"))
    return jax.shard_map(body, mesh=mesh, in_specs=in_specs, out_specs=out_specs, check_vma=False)
```

```python
import functools
import math

import jax
import jax.numpy as jnp
from jax import lax
from jax.experimental import pallas as pl
from jax.experimental.pallas import tpu as pltpu
from jax.sharding import PartitionSpec as P

VMEM_SPEC = pl.BlockSpec(memory_space=pltpu.VMEM)
SMEM_SPEC = pl.BlockSpec(memory_space=pltpu.SMEM)
ANY_SPEC = pl.BlockSpec(memory_space=pl.ANY)
MASKED = -1e30
ROW_SLOTS = 2


def in_hbm(value):
    return pltpu.with_memory_space_constraint(value, pltpu.HBM)


def tile_copies(source, first, out, sem):
    chunks = sem.shape[1]
    part = source.shape[1] // chunks
    return [
        pltpu.make_async_copy(
            source.at[0, pl.ds(c * part, part), :, pl.ds((first + t) * 128, 128)],
            out.at[t, pl.ds(c * part, part)],
            sem.at[t, c],
        )
        for c in range(chunks)
        for t in range(out.shape[0])
    ]


def attention_kernel(
    selected_in,
    queries_in,
    new_key_in,
    new_value_in,
    centroid_keys,
    centroid_values,
    key_cache,
    value_cache,
    weight_in,
    out,
    weight_out,
    selected,
    queries,
    new_key,
    new_value,
    keys,
    values,
    small_sem,
    picked_sem,
):
    seq_count, heads_kv, query_count, head_dim = queries.shape
    centroid_rows = centroid_keys.shape[1]
    clusters = centroid_rows // heads_kv
    sel_count = selected.shape[1]
    block_rows = key_cache.shape[1] // clusters
    ctx_pos = lax.axis_index("ctx")
    pairs = (
        (selected_in, selected),
        (centroid_keys, keys.at[:, pl.ds(0, centroid_rows)]),
        (queries_in, queries),
        (new_key_in, new_key),
        (new_value_in, new_value),
        (centroid_values, values.at[:, pl.ds(0, centroid_rows)]),
        (weight_in, weight_out),
    )
    small = [
        pltpu.make_async_copy(source, held, small_sem.at[i]) for i, (source, held) in enumerate(pairs)
    ]
    for copy in small:
        copy.start()
    small[0].wait()
    picked = ([], [])
    for which, (source, held) in enumerate(((key_cache, keys), (value_cache, values))):
        for s in range(seq_count):
            for g in range(heads_kv):
                for j in range(sel_count):
                    block = selected[g, j, s] - ctx_pos * clusters
                    start = pl.multiple_of(block * block_rows, block_rows)
                    place = centroid_rows + (g * sel_count + j) * block_rows
                    copy = pltpu.make_async_copy(
                        source.at[s, pl.ds(start, block_rows)],
                        held.at[s, pl.ds(place, block_rows)],
                        picked_sem.at[which, s, g * sel_count + j],
                    )
                    copy.start()
                    picked[which].append(copy)
    heads = heads_kv * query_count
    score_scale = 1.0 / math.sqrt(head_dim)

    def scored(first, count, valid):
        part = [
            lax.dot_general(
                queries[s].reshape(heads, head_dim),
                keys[s, first : first + count],
                (((1,), (1,)), ((), ())),
                preferred_element_type=jnp.float32,
            )
            for s in range(seq_count)
        ]
        return jnp.where(valid, jnp.concatenate(part, axis=0) * score_scale, MASKED)

    picked_rows = keys.shape[1] - centroid_rows
    shape = (seq_count * heads, centroid_rows)
    head_of_query = lax.broadcasted_iota(jnp.int32, shape, 0) // query_count % heads_kv
    same_head = lax.broadcasted_iota(jnp.int32, shape, 1) % heads_kv == head_of_query
    shape = (seq_count * heads, picked_rows)
    head_of_query = lax.broadcasted_iota(jnp.int32, shape, 0) // query_count % heads_kv
    column = lax.broadcasted_iota(jnp.int32, shape, 1)
    same_block = (column % heads_kv == head_of_query) & (
        column // (sel_count * block_rows) == head_of_query
    )
    for copy in small[1:4]:
        copy.wait()
    own = []
    for s in range(seq_count):
        products = queries[s].astype(jnp.float32) * new_key[s].astype(jnp.float32)[:, None, :]
        own.append(jnp.sum(products, axis=-1, keepdims=True).reshape(heads, 1))
    own = jnp.where(ctx_pos == 0, jnp.concatenate(own, axis=0) * score_scale, MASKED)
    to_centroids = scored(0, centroid_rows, same_head)
    peak = jnp.maximum(jnp.max(to_centroids, axis=-1, keepdims=True), own)
    for copy in picked[0]:
        copy.wait()
    to_picked = scored(centroid_rows, picked_rows, same_block)
    peak = jnp.maximum(jnp.max(to_picked, axis=-1, keepdims=True), peak)
    probs = jnp.exp(jnp.concatenate([to_centroids, to_picked], axis=1) - peak)
    own_prob = jnp.exp(own - peak)
    total = jnp.sum(probs, axis=-1, keepdims=True) + own_prob
    probs = probs.astype(jnp.bfloat16)
    lane = lax.broadcasted_iota(jnp.int32, (seq_count * heads, head_dim), 1)
    stats = jnp.where(lane < head_dim // 2, peak, total)
    for copy in small[4:6] + picked[1]:
        copy.wait()
    for s in range(seq_count):
        mine = slice(s * heads, (s + 1) * heads)
        weighted = jnp.dot(probs[mine], values[s], preferred_element_type=jnp.float32)
        own_value = jnp.broadcast_to(
            new_value[s].astype(jnp.float32)[:, None, :], (heads_kv, query_count, head_dim)
        ).reshape(heads, head_dim)
        weighted = weighted + own_prob[mine] * own_value
        for g in range(heads_kv):
            part = slice(g * query_count, (g + 1) * query_count)
            out[:, g * seq_count + s, :] = weighted[part]
            out[:, (heads_kv + g) * seq_count + s, :] = stats[mine][part]
    small[6].wait()


def attention(
    queries, key_cache, value_cache, centroid_keys, centroid_values, selected, new_key, new_value, weight
):
    seq_count, heads_kv, query_count, head_dim = queries.shape
    clusters = centroid_keys.shape[1]
    sel_count = selected.shape[2]
    block_rows = key_cache.shape[1] // clusters * heads_kv
    selected = selected.transpose(1, 2, 0)
    centroid_keys, centroid_values, key_cache, value_cache = (
        value.reshape(seq_count, -1, head_dim)
        for value in (centroid_keys, centroid_values, key_cache, value_cache)
    )
    held_rows = clusters * heads_kv + heads_kv * sel_count * block_rows
    held = pltpu.VMEM((seq_count, held_rows, head_dim), jnp.bfloat16)
    operands = (
        selected, queries, new_key, new_value, centroid_keys, centroid_values, key_cache, value_cache, weight
    )
    return pl.pallas_call(
        attention_kernel,
        out_shape=(
            pltpu.VMEM((query_count, 2 * heads_kv * seq_count, head_dim), jnp.float32),
            pltpu.VMEM(weight.shape, weight.dtype),
        ),
        in_specs=[ANY_SPEC] * 9,
        out_specs=(VMEM_SPEC, VMEM_SPEC),
        scratch_shapes=[
            pltpu.SMEM(selected.shape, selected.dtype),
            pltpu.VMEM(queries.shape, queries.dtype),
            pltpu.VMEM(new_key.shape, new_key.dtype),
            pltpu.VMEM(new_value.shape, new_value.dtype),
            held,
            held,
            pltpu.SemaphoreType.DMA((7,)),
            pltpu.SemaphoreType.DMA((2, seq_count, heads_kv * sel_count)),
        ],
        compiler_params=pltpu.CompilerParams(vmem_limit_bytes=12 << 20),
    )(*[in_hbm(operand) for operand in operands])


def project_kernel(parts, weight, out):
    rows = parts.shape[1] // 2
    half = parts.shape[2] // 2
    weighted = parts[:, :rows, :]
    peak = parts[:, rows:, 0:1]
    total = parts[:, rows:, half : half + 1]
    scale = jnp.exp(peak - jnp.max(peak, axis=0, keepdims=True))
    total = jnp.sum(total * scale, axis=0)
    attended = (jnp.sum(weighted * scale, axis=0) / total).astype(jnp.bfloat16)
    seq_count = out.shape[0]
    attended = jnp.concatenate(
        [attended[first : first + seq_count] for first in range(0, rows, seq_count)], axis=1
    )
    sums = jnp.dot(attended, weight[...], preferred_element_type=jnp.float32)
    out[...] = sums.astype(jnp.bfloat16)


def project(parts, weight):
    seq_count = parts.shape[1] * parts.shape[2] // (2 * weight.shape[0])
    return pl.pallas_call(
        project_kernel,
        out_shape=jax.ShapeDtypeStruct((seq_count, weight.shape[1]), jnp.bfloat16),
        in_specs=[VMEM_SPEC, VMEM_SPEC],
        out_specs=VMEM_SPEC,
        compiler_params=pltpu.CompilerParams(vmem_limit_bytes=8 << 20),
    )(parts, weight)


def fetch_kernel(first, source, *refs):
    out, sem = refs[-2:]
    copies = tile_copies(source, first, out, sem)
    for copy in copies:
        copy.start()
    for copy in copies:
        copy.wait()


def fetch(weights, first, count, *after):
    depth = weights.shape[1]
    tiles = pl.pallas_call(
        functools.partial(fetch_kernel, first),
        out_shape=pltpu.VMEM((count, depth, 2, 128), weights.dtype),
        in_specs=[ANY_SPEC] * (1 + len(after)),
        out_specs=VMEM_SPEC,
        scratch_shapes=[pltpu.SemaphoreType.DMA((count, 4))],
        compiler_params=pltpu.CompilerParams(vmem_limit_bytes=1 << 20),
        cost_estimate=pl.CostEstimate(
            flops=0, bytes_accessed=count * depth * 512, transcendentals=0
        ),
    )(in_hbm(weights), *after)
    return tiles.reshape(count, 2 * depth, 128)


def spread_rows(x, model_dim, spread):
    rows = x.shape[0]
    source = lax.broadcasted_iota(jnp.int32, (128, 512), 0)
    target = lax.broadcasted_iota(jnp.int32, (128, 512), 1)
    ends = (target == 2 * source) | (target == 2 * source + 257)
    to_both = jnp.where(ends, 1.0, 0.0).astype(jnp.bfloat16)
    pieces = [x[:, j * 128 : (j + 1) * 128] for j in range(model_dim // 128)]
    result = jnp.dot(
        jnp.concatenate(pieces, axis=0), to_both, preferred_element_type=jnp.float32
    ).astype(jnp.bfloat16)
    for j in range(model_dim // 128):
        columns = slice(j * 256, (j + 1) * 256)
        spread[0:rows, columns] = result[j * rows : (j + 1) * rows, 0:256]
        spread[rows : 2 * rows, columns] = result[j * rows : (j + 1) * rows, 256:512]


def spread_kernel(x, spread):
    spread_rows(x, spread.shape[1] // 2, spread)


def spread_alone(x, model_dim):
    return pl.pallas_call(
        spread_kernel,
        out_shape=pltpu.VMEM((2 * x.shape[0], 2 * model_dim), x.dtype),
        in_specs=[VMEM_SPEC],
        out_specs=VMEM_SPEC,
        compiler_params=pltpu.CompilerParams(vmem_limit_bytes=4 << 20),
        cost_estimate=pl.CostEstimate(flops=0, bytes_accessed=1 << 20, transcendentals=0),
    )(x)


def experts_kernel(order, x0, x1, first, *refs):
    *tiles, down, out, second = refs
    half = x0.shape[0]
    model_dim = second.shape[1] // 2
    rows = 2 * half
    blocks = len(order)
    seq_count = rows // blocks
    slots = out.shape[1] // 2
    exp_pos = lax.axis_index("exp")
    names = jnp.concatenate([x0[:, model_dim:], x1[:, model_dim:]], axis=0).astype(jnp.float32)
    lane = lax.broadcasted_iota(jnp.int32, names.shape, 1)
    here = lax.axis_index("ctx") * blocks + exp_pos
    code = jnp.sum(jnp.where(lane == here, names, 0.0), axis=-1, keepdims=True)
    row = lax.broadcasted_iota(jnp.int32, names.shape, 0)
    place = row // seq_count * slots + code.astype(jnp.int32) - 1
    chosen = jnp.where((code > 0.5) & (place == lane), 1.0, 0.0)
    chosen = chosen.T[: blocks * slots].astype(jnp.bfloat16)
    spread_rows(x1, model_dim, second)
    lanes = [tile.at[t] for tile in tiles for t in range(tile.shape[0])]
    depth = 1024
    both = []
    for u in range(len(lanes) // 2):
        total = jnp.zeros((2 * rows, 256), jnp.float32)
        for c in range(2 * model_dim // depth):
            here = slice(c * depth, (c + 1) * depth)
            right = jnp.concatenate([lanes[2 * u][here, :], lanes[2 * u + 1][here, :]], axis=1)
            left = jnp.concatenate([first[:, here], second[:, here]], axis=0)
            total = total + jnp.dot(left, right, preferred_element_type=jnp.float32)
        both.append(total)
    both = jnp.concatenate(both, axis=1)
    gate = jnp.concatenate([both[0:half], both[rows : rows + half]], axis=0)
    up = jnp.concatenate([both[half:rows], both[rows + half :]], axis=0)
    activated = (jax.nn.silu(gate) * up).astype(jnp.bfloat16)
    activated = jnp.dot(chosen, activated, preferred_element_type=jnp.float32).astype(jnp.bfloat16)
    width = 2048

    def down_part(b, carry):
        columns = pl.ds(pl.multiple_of(b * width, width), width)
        result = jnp.dot(
            activated, down[0, :, columns], preferred_element_type=jnp.float32
        ).astype(jnp.bfloat16)
        for q in range(width // 256):
            for p, i in enumerate(order):
                place = (b * (width // 256) + q) * blocks + lax.bitwise_xor(exp_pos, i)
                mine = result[p * slots : (p + 1) * slots]
                out[place, 0:slots] = mine[:, q * 256 : q * 256 + 128]
                out[place, slots : 2 * slots] = mine[:, q * 256 + 128 : (q + 1) * 256]
        return carry

    lax.fori_loop(0, model_dim // width, down_part, 0)


def experts(pieces, tiles, down, order, slots):
    half = pieces[0].shape[0]
    model_dim = down.shape[2]
    rows = 2 * half
    blocks = len(order)
    return pl.pallas_call(
        functools.partial(experts_kernel, order),
        out_shape=pltpu.VMEM((model_dim // 256 * blocks, 2 * slots, 128), jnp.bfloat16),
        in_specs=[VMEM_SPEC] * (4 + len(tiles)),
        out_specs=VMEM_SPEC,
        scratch_shapes=[pltpu.VMEM((rows, 2 * model_dim), jnp.bfloat16)],
        compiler_params=pltpu.CompilerParams(vmem_limit_bytes=16 << 20),
    )(*pieces, spread_alone(pieces[0], model_dim), *tiles, down)


def sum_kernel(p0, p1, p2, p3, before, out):
    total = p0[...].astype(jnp.float32)
    for piece in (p1, p2, p3):
        total = total + piece[...].astype(jnp.float32)
    out[...] = total.astype(out.dtype)


def sum_pieces(pieces, before):
    return pl.pallas_call(
        sum_kernel,
        out_shape=pltpu.VMEM(pieces[0].shape, pieces[0].dtype),
        in_specs=[VMEM_SPEC] * 4 + [ANY_SPEC],
        out_specs=VMEM_SPEC,
        compiler_params=pltpu.CompilerParams(vmem_limit_bytes=2 << 20),
    )(*pieces, before)


def norm_kernel(kvh_devices, p0, p1, p2, p3, residual, gain, ids, before, own, normed):
    total = residual[...].astype(jnp.float32)
    for piece in (p0, p1, p2, p3):
        total = total + piece[...].astype(jnp.float32)
    seq_count, model_dim = total.shape
    mean_square = jnp.mean(total * total, axis=-1, keepdims=True)
    rows = total * lax.rsqrt(mean_square + 1e-06) * gain[...]
    normed[:, :model_dim] = rows.astype(normed.dtype)
    lane = lax.broadcasted_iota(jnp.int32, (seq_count, normed.shape[1] - model_dim), 1)
    names = jnp.zeros(lane.shape, jnp.float32)
    for k in range(ids.shape[1]):
        names = jnp.where(ids[:, k : k + 1] == lane, 1.0, names)
    slot = [names[0:1]]
    for r in range(1, seq_count):
        slot.append(slot[-1] + names[r : r + 1])
    normed[:, model_dim:] = (names * jnp.concatenate(slot, axis=0)).astype(normed.dtype)
    place = lax.axis_index("ctx") * kvh_devices + lax.axis_index("kvh")
    width = own.shape[1]
    for p in range(model_dim // width):
        @pl.when(place == p)
        def _():
            own[...] = total[:, p * width : (p + 1) * width]


def norm(pieces, residual, gain, ids, before, kvh_devices):
    seq_count, model_dim = residual.shape
    return pl.pallas_call(
        functools.partial(norm_kernel, kvh_devices),
        out_shape=(
            pltpu.VMEM((seq_count, 256), jnp.float32),
            pltpu.VMEM((seq_count, model_dim + 128), jnp.bfloat16),
        ),
        in_specs=[VMEM_SPEC] * 7 + [ANY_SPEC],
        out_specs=(VMEM_SPEC,) * 2,
        compiler_params=pltpu.CompilerParams(vmem_limit_bytes=2 << 20),
    )(*pieces, residual, gain.reshape(1, -1), ids, before)


def weights_kernel(sizes, ids, gates, after, mix):
    kvh_devices, exp_devices, slots = sizes
    seq_count = ids.shape[0]
    shape = (seq_count, mix.shape[1])
    column = lax.broadcasted_iota(jnp.int32, shape, 1)
    device = column // (2 * slots)
    expert = device // (kvh_devices * exp_devices) * exp_devices + device % exp_devices
    weight = jnp.zeros(shape, jnp.float32)
    named = jnp.zeros(shape, jnp.float32)
    for k in range(ids.shape[1]):
        match = ids[:, k : k + 1] == expert
        weight = jnp.where(match, gates[:, k : k + 1], weight)
        named = jnp.where(match, 1.0, named)
    rank = [jnp.zeros((1, shape[1]), jnp.float32)]
    for r in range(seq_count - 1):
        rank.append(rank[-1] + named[r : r + 1])
    rank = jnp.concatenate(rank, axis=0)
    slot = (column % slots).astype(jnp.float32)
    weight = jnp.where(jnp.abs(rank - slot) < 0.5, weight, 0.0)
    half = column // slots % 2
    weight = jnp.concatenate([jnp.where(half == h, weight, 0.0) for h in range(2)], axis=0)
    high = weight.astype(jnp.bfloat16)
    mix[0 : 2 * seq_count] = high
    mix[2 * seq_count : 4 * seq_count] = (weight - high.astype(jnp.float32)).astype(jnp.bfloat16)


def mixing_weights(ids, gates, after, sizes, devices):
    slots = sizes[2]
    return pl.pallas_call(
        functools.partial(weights_kernel, sizes),
        out_shape=pltpu.VMEM((4 * ids.shape[0], devices * 2 * slots), jnp.bfloat16),
        in_specs=[VMEM_SPEC] * 2 + [ANY_SPEC],
        out_specs=VMEM_SPEC,
        compiler_params=pltpu.CompilerParams(vmem_limit_bytes=2 << 20),
    )(ids, gates, after)


def stack_kernel(p0, p1, p2, p3, before, out):
    out[...] = jnp.concatenate([p0[...], p1[...], p2[...], p3[...]], axis=0)


def stack(pieces, before):
    rows, columns = pieces[0].shape
    return pl.pallas_call(
        stack_kernel,
        out_shape=pltpu.VMEM((4 * rows, columns), pieces[0].dtype),
        in_specs=[VMEM_SPEC] * 4 + [ANY_SPEC],
        out_specs=VMEM_SPEC,
        compiler_params=pltpu.CompilerParams(vmem_limit_bytes=2 << 20),
    )(*pieces, before)


def mix_kernel(returned, mix, own, out):
    seq_count = own.shape[0]
    sums = jnp.dot(mix[...], returned[...], preferred_element_type=jnp.float32)
    sums = sums[0 : 2 * seq_count] + sums[2 * seq_count : 4 * seq_count]
    width = sums.shape[1]
    out[:, 0:width] = (own[:, 0:width] + sums[0:seq_count]).astype(out.dtype)
    out[:, width : 2 * width] = (own[:, width : 2 * width] + sums[seq_count:]).astype(out.dtype)


def mix_results(returned, mix, own):
    return pl.pallas_call(
        mix_kernel,
        out_shape=jax.ShapeDtypeStruct(own.shape, jnp.bfloat16),
        in_specs=[VMEM_SPEC] * 3,
        out_specs=VMEM_SPEC,
        compiler_params=pltpu.CompilerParams(vmem_limit_bytes=2 << 20),
    )(returned.reshape(-1, returned.shape[2]), mix, own)


def swapped(value, axes, count, mask):
    return lax.ppermute(value, axes, [(i, i ^ mask) for i in range(count)])


def body(
    queries,
    key_cache,
    value_cache,
    centroid_keys,
    centroid_values,
    selected,
    new_key,
    new_value,
    out_weight,
    residual,
    norm_gain,
    expert_ids,
    gate_weights,
    w_gate_up,
    w_down,
):
    ctx_devices = lax.axis_size("ctx")
    kvh_devices = lax.axis_size("kvh")
    exp_devices = lax.axis_size("exp")
    plane = ctx_devices * kvh_devices

    parts, out_weight = attention(
        queries,
        key_cache,
        value_cache,
        centroid_keys,
        centroid_values,
        selected,
        new_key,
        new_value,
        out_weight.reshape(-1, out_weight.shape[3]),
    )
    parts = lax.all_to_all(parts, "ctx", split_axis=0, concat_axis=0, tiled=True)

    projected = project(parts, out_weight)

    axes = ("ctx", "kvh")
    along_x = [projected] + [swapped(projected, axes, plane, m) for m in (2, 3, 1)]
    tiles = [fetch(w_gate_up, 0, 2, projected)]
    sums = sum_pieces(along_x, tiles[-1])
    along_z = [sums] + [swapped(sums, axes, plane, m) for m in (4, 12, 8)]
    tiles.append(fetch(w_gate_up, 2, 2, sums))
    own, normed = norm(along_z, residual, norm_gain, expert_ids, tiles[-1], kvh_devices)

    steps = (0, 2, 6, 4)
    along_y = [normed] + [swapped(normed, "exp", exp_devices, m) for m in steps[1:]]
    tiles.append(fetch(w_gate_up, 4, 2, normed))
    mine = stack(along_y, tiles[-1])
    other = swapped(mine, "exp", exp_devices, 1)
    order = steps + tuple(m + 1 for m in steps)
    results = experts((mine, other), tiles, w_down, order, ROW_SLOTS)
    returned = lax.all_to_all(
        results, ("ctx", "kvh", "exp"), split_axis=0, concat_axis=0, tiled=True
    )
    sizes = (kvh_devices, exp_devices, ROW_SLOTS)
    mix = mixing_weights(expert_ids, gate_weights, results, sizes, plane * exp_devices)
    return mix_results(returned, mix, own)


def solution(mesh):
    in_specs = (
        P("exp", "kvh", None, None),
        P("exp", "ctx", "kvh", None),
        P("exp", "ctx", "kvh", None),
        P("exp", "ctx", "kvh", None),
        P("exp", "ctx", "kvh", None),
        P("exp", "kvh", "ctx"),
        P("exp", "kvh", None),
        P("exp", "kvh", None),
        P("kvh", "ctx", None, None),
        P("exp", None),
        P(),
        P("exp", None),
        P("exp", None),
        P(("ctx", "exp"), None, None, "kvh"),
        P(("ctx", "exp"), "kvh", None),
    )
    out_specs = P("exp", ("ctx", "kvh"))
    return jax.shard_map(body, mesh=mesh, in_specs=in_specs, out_specs=out_specs, check_vma=False)
```

```python
import functools
import math

import jax
import jax.numpy as jnp
from jax import lax
from jax.experimental import pallas as pl
from jax.experimental.pallas import tpu as pltpu
from jax.sharding import PartitionSpec as P

VMEM_SPEC = pl.BlockSpec(memory_space=pltpu.VMEM)
SMEM_SPEC = pl.BlockSpec(memory_space=pltpu.SMEM)
ANY_SPEC = pl.BlockSpec(memory_space=pl.ANY)
MASKED = -1e30
ROW_SLOTS = 2


def in_hbm(value):
    return pltpu.with_memory_space_constraint(value, pltpu.HBM)


def tile_copies(source, first, out, sem):
    chunks = sem.shape[1]
    part = source.shape[1] // chunks
    return [
        pltpu.make_async_copy(
            source.at[0, pl.ds(c * part, part), :, pl.ds((first + t) * 128, 128)],
            out.at[t, pl.ds(c * part, part)],
            sem.at[t, c],
        )
        for c in range(chunks)
        for t in range(out.shape[0])
    ]


def attention_kernel(
    selected_in,
    queries_in,
    new_key_in,
    new_value_in,
    centroid_keys,
    centroid_values,
    key_cache,
    value_cache,
    weight_in,
    out,
    weight_out,
    selected,
    queries,
    new_key,
    new_value,
    keys,
    values,
    small_sem,
    picked_sem,
):
    seq_count, heads_kv, query_count, head_dim = queries.shape
    centroid_rows = centroid_keys.shape[1]
    clusters = centroid_rows // heads_kv
    sel_count = selected.shape[1]
    block_rows = key_cache.shape[1] // clusters
    ctx_pos = lax.axis_index("ctx")
    pairs = (
        (selected_in, selected),
        (centroid_keys, keys.at[:, pl.ds(0, centroid_rows)]),
        (queries_in, queries),
        (new_key_in, new_key),
        (new_value_in, new_value),
        (centroid_values, values.at[:, pl.ds(0, centroid_rows)]),
        (weight_in, weight_out),
    )
    small = [
        pltpu.make_async_copy(source, held, small_sem.at[i]) for i, (source, held) in enumerate(pairs)
    ]
    for copy in small:
        copy.start()
    small[0].wait()
    picked = ([], [])
    for which, (source, held) in enumerate(((key_cache, keys), (value_cache, values))):
        for s in range(seq_count):
            for g in range(heads_kv):
                for j in range(sel_count):
                    block = selected[g, j, s] - ctx_pos * clusters
                    start = pl.multiple_of(block * block_rows, block_rows)
                    place = centroid_rows + (g * sel_count + j) * block_rows
                    copy = pltpu.make_async_copy(
                        source.at[s, pl.ds(start, block_rows)],
                        held.at[s, pl.ds(place, block_rows)],
                        picked_sem.at[which, s, g * sel_count + j],
                    )
                    copy.start()
                    picked[which].append(copy)
    heads = heads_kv * query_count
    score_scale = 1.0 / math.sqrt(head_dim)

    def scored(first, count, valid):
        part = [
            lax.dot_general(
                queries[s].reshape(heads, head_dim),
                keys[s, first : first + count],
                (((1,), (1,)), ((), ())),
                preferred_element_type=jnp.float32,
            )
            for s in range(seq_count)
        ]
        return jnp.where(valid, jnp.concatenate(part, axis=0) * score_scale, MASKED)

    picked_rows = keys.shape[1] - centroid_rows
    shape = (seq_count * heads, centroid_rows)
    head_of_query = lax.broadcasted_iota(jnp.int32, shape, 0) // query_count % heads_kv
    same_head = lax.broadcasted_iota(jnp.int32, shape, 1) % heads_kv == head_of_query
    shape = (seq_count * heads, picked_rows)
    head_of_query = lax.broadcasted_iota(jnp.int32, shape, 0) // query_count % heads_kv
    column = lax.broadcasted_iota(jnp.int32, shape, 1)
    same_block = (column % heads_kv == head_of_query) & (
        column // (sel_count * block_rows) == head_of_query
    )
    for copy in small[1:4]:
        copy.wait()
    own = []
    for s in range(seq_count):
        products = queries[s].astype(jnp.float32) * new_key[s].astype(jnp.float32)[:, None, :]
        own.append(jnp.sum(products, axis=-1, keepdims=True).reshape(heads, 1))
    own = jnp.where(ctx_pos == 0, jnp.concatenate(own, axis=0) * score_scale, MASKED)
    to_centroids = scored(0, centroid_rows, same_head)
    peak = jnp.maximum(jnp.max(to_centroids, axis=-1, keepdims=True), own)
    for copy in picked[0]:
        copy.wait()
    to_picked = scored(centroid_rows, picked_rows, same_block)
    peak = jnp.maximum(jnp.max(to_picked, axis=-1, keepdims=True), peak)
    probs = jnp.exp(jnp.concatenate([to_centroids, to_picked], axis=1) - peak)
    own_prob = jnp.exp(own - peak)
    total = jnp.sum(probs, axis=-1, keepdims=True) + own_prob
    probs = probs.astype(jnp.bfloat16)
    lane = lax.broadcasted_iota(jnp.int32, (seq_count * heads, head_dim), 1)
    stats = jnp.where(lane < head_dim // 2, peak, total)
    for copy in small[4:6] + picked[1]:
        copy.wait()
    for s in range(seq_count):
        mine = slice(s * heads, (s + 1) * heads)
        weighted = jnp.dot(probs[mine], values[s], preferred_element_type=jnp.float32)
        own_value = jnp.broadcast_to(
            new_value[s].astype(jnp.float32)[:, None, :], (heads_kv, query_count, head_dim)
        ).reshape(heads, head_dim)
        weighted = weighted + own_prob[mine] * own_value
        for g in range(heads_kv):
            part = slice(g * query_count, (g + 1) * query_count)
            out[:, g * seq_count + s, :] = weighted[part]
            out[:, (heads_kv + g) * seq_count + s, :] = stats[mine][part]
    small[6].wait()


def attention(
    queries, key_cache, value_cache, centroid_keys, centroid_values, selected, new_key, new_value, weight
):
    seq_count, heads_kv, query_count, head_dim = queries.shape
    clusters = centroid_keys.shape[1]
    sel_count = selected.shape[2]
    block_rows = key_cache.shape[1] // clusters * heads_kv
    selected = selected.transpose(1, 2, 0)
    centroid_keys, centroid_values, key_cache, value_cache = (
        value.reshape(seq_count, -1, head_dim)
        for value in (centroid_keys, centroid_values, key_cache, value_cache)
    )
    held_rows = clusters * heads_kv + heads_kv * sel_count * block_rows
    held = pltpu.VMEM((seq_count, held_rows, head_dim), jnp.bfloat16)
    operands = (
        selected, queries, new_key, new_value, centroid_keys, centroid_values, key_cache, value_cache, weight
    )
    return pl.pallas_call(
        attention_kernel,
        out_shape=(
            pltpu.VMEM((query_count, 2 * heads_kv * seq_count, head_dim), jnp.float32),
            pltpu.VMEM(weight.shape, weight.dtype),
        ),
        in_specs=[ANY_SPEC] * 9,
        out_specs=(VMEM_SPEC, VMEM_SPEC),
        scratch_shapes=[
            pltpu.SMEM(selected.shape, selected.dtype),
            pltpu.VMEM(queries.shape, queries.dtype),
            pltpu.VMEM(new_key.shape, new_key.dtype),
            pltpu.VMEM(new_value.shape, new_value.dtype),
            held,
            held,
            pltpu.SemaphoreType.DMA((7,)),
            pltpu.SemaphoreType.DMA((2, seq_count, heads_kv * sel_count)),
        ],
        compiler_params=pltpu.CompilerParams(vmem_limit_bytes=12 << 20),
    )(*[in_hbm(operand) for operand in operands])


def project_kernel(parts, weight, out):
    rows = parts.shape[1] // 2
    half = parts.shape[2] // 2
    weighted = parts[:, :rows, :]
    peak = parts[:, rows:, 0:1]
    total = parts[:, rows:, half : half + 1]
    scale = jnp.exp(peak - jnp.max(peak, axis=0, keepdims=True))
    total = jnp.sum(total * scale, axis=0)
    attended = (jnp.sum(weighted * scale, axis=0) / total).astype(jnp.bfloat16)
    seq_count = out.shape[0]
    attended = jnp.concatenate(
        [attended[first : first + seq_count] for first in range(0, rows, seq_count)], axis=1
    )
    sums = jnp.dot(attended, weight[...], preferred_element_type=jnp.float32)
    out[...] = sums.astype(jnp.bfloat16)


def project(parts, weight):
    seq_count = parts.shape[1] * parts.shape[2] // (2 * weight.shape[0])
    return pl.pallas_call(
        project_kernel,
        out_shape=jax.ShapeDtypeStruct((seq_count, weight.shape[1]), jnp.bfloat16),
        in_specs=[VMEM_SPEC, VMEM_SPEC],
        out_specs=VMEM_SPEC,
        compiler_params=pltpu.CompilerParams(vmem_limit_bytes=8 << 20),
    )(parts, weight)


def fetch_kernel(first, source, *refs):
    out, sem = refs[-2:]
    copies = tile_copies(source, first, out, sem)
    for copy in copies:
        copy.start()
    for copy in copies:
        copy.wait()


def fetch(weights, first, count, *after):
    depth = weights.shape[1]
    tiles = pl.pallas_call(
        functools.partial(fetch_kernel, first),
        out_shape=pltpu.VMEM((count, depth, 2, 128), weights.dtype),
        in_specs=[ANY_SPEC] * (1 + len(after)),
        out_specs=VMEM_SPEC,
        scratch_shapes=[pltpu.SemaphoreType.DMA((count, 4))],
        compiler_params=pltpu.CompilerParams(vmem_limit_bytes=1 << 20),
        cost_estimate=pl.CostEstimate(
            flops=0, bytes_accessed=count * depth * 512, transcendentals=0
        ),
    )(in_hbm(weights), *after)
    return tiles.reshape(count, 2 * depth, 128)


def spread_rows(x, model_dim, spread):
    rows = x.shape[0]
    source = lax.broadcasted_iota(jnp.int32, (128, 512), 0)
    target = lax.broadcasted_iota(jnp.int32, (128, 512), 1)
    ends = (target == 2 * source) | (target == 2 * source + 257)
    to_both = jnp.where(ends, 1.0, 0.0).astype(jnp.bfloat16)
    pieces = [x[:, j * 128 : (j + 1) * 128] for j in range(model_dim // 128)]
    result = jnp.dot(
        jnp.concatenate(pieces, axis=0), to_both, preferred_element_type=jnp.float32
    ).astype(jnp.bfloat16)
    for j in range(model_dim // 128):
        columns = slice(j * 256, (j + 1) * 256)
        spread[0:rows, columns] = result[j * rows : (j + 1) * rows, 0:256]
        spread[rows : 2 * rows, columns] = result[j * rows : (j + 1) * rows, 256:512]


def spread_kernel(x, spread):
    spread_rows(x, spread.shape[1] // 2, spread)


def spread_alone(x, model_dim):
    return pl.pallas_call(
        spread_kernel,
        out_shape=pltpu.VMEM((2 * x.shape[0], 2 * model_dim), x.dtype),
        in_specs=[VMEM_SPEC],
        out_specs=VMEM_SPEC,
        compiler_params=pltpu.CompilerParams(vmem_limit_bytes=4 << 20),
        cost_estimate=pl.CostEstimate(flops=0, bytes_accessed=1 << 20, transcendentals=0),
    )(x)


def experts_kernel(order, x0, x1, first, *refs):
    *tiles, down, out, second = refs
    half = x0.shape[0]
    model_dim = second.shape[1] // 2
    rows = 2 * half
    blocks = len(order)
    seq_count = rows // blocks
    slots = out.shape[1] // 2
    exp_pos = lax.axis_index("exp")
    names = jnp.concatenate([x0[:, model_dim:], x1[:, model_dim:]], axis=0).astype(jnp.float32)
    lane = lax.broadcasted_iota(jnp.int32, names.shape, 1)
    here = lax.axis_index("ctx") * blocks + exp_pos
    code = jnp.sum(jnp.where(lane == here, names, 0.0), axis=-1, keepdims=True)
    row = lax.broadcasted_iota(jnp.int32, names.shape, 0)
    place = row // seq_count * slots + code.astype(jnp.int32) - 1
    chosen = jnp.where((code > 0.5) & (place == lane), 1.0, 0.0)
    chosen = chosen.T[: blocks * slots].astype(jnp.bfloat16)
    spread_rows(x1, model_dim, second)
    lanes = [tile.at[t] for tile in tiles for t in range(tile.shape[0])]
    depth = 1024
    both = []
    for u in range(len(lanes) // 2):
        total = jnp.zeros((2 * rows, 256), jnp.float32)
        for c in range(2 * model_dim // depth):
            here = slice(c * depth, (c + 1) * depth)
            right = jnp.concatenate([lanes[2 * u][here, :], lanes[2 * u + 1][here, :]], axis=1)
            left = jnp.concatenate([first[:, here], second[:, here]], axis=0)
            total = total + jnp.dot(left, right, preferred_element_type=jnp.float32)
        both.append(total)
    both = jnp.concatenate(both, axis=1)
    gate = jnp.concatenate([both[0:half], both[rows : rows + half]], axis=0)
    up = jnp.concatenate([both[half:rows], both[rows + half :]], axis=0)
    activated = (jax.nn.silu(gate) * up).astype(jnp.bfloat16)
    activated = jnp.dot(chosen, activated, preferred_element_type=jnp.float32).astype(jnp.bfloat16)
    width = 2048

    def down_part(b, carry):
        columns = pl.ds(pl.multiple_of(b * width, width), width)
        result = jnp.dot(
            activated, down[0, :, columns], preferred_element_type=jnp.float32
        ).astype(jnp.bfloat16)
        for q in range(width // 256):
            for p, i in enumerate(order):
                place = (b * (width // 256) + q) * blocks + lax.bitwise_xor(exp_pos, i)
                mine = result[p * slots : (p + 1) * slots]
                out[place, 0:slots] = mine[:, q * 256 : q * 256 + 128]
                out[place, slots : 2 * slots] = mine[:, q * 256 + 128 : (q + 1) * 256]
        return carry

    lax.fori_loop(0, model_dim // width, down_part, 0)


def experts(pieces, tiles, down, order, slots):
    half = pieces[0].shape[0]
    model_dim = down.shape[2]
    rows = 2 * half
    blocks = len(order)
    return pl.pallas_call(
        functools.partial(experts_kernel, order),
        out_shape=pltpu.VMEM((model_dim // 256 * blocks, 2 * slots, 128), jnp.bfloat16),
        in_specs=[VMEM_SPEC] * (4 + len(tiles)),
        out_specs=VMEM_SPEC,
        scratch_shapes=[pltpu.VMEM((rows, 2 * model_dim), jnp.bfloat16)],
        compiler_params=pltpu.CompilerParams(vmem_limit_bytes=16 << 20),
    )(*pieces, spread_alone(pieces[0], model_dim), *tiles, down)


def sum_kernel(p0, p1, p2, p3, before, out):
    total = p0[...].astype(jnp.float32)
    for piece in (p1, p2, p3):
        total = total + piece[...].astype(jnp.float32)
    out[...] = total.astype(out.dtype)


def sum_pieces(pieces, before):
    return pl.pallas_call(
        sum_kernel,
        out_shape=pltpu.VMEM(pieces[0].shape, pieces[0].dtype),
        in_specs=[VMEM_SPEC] * 4 + [ANY_SPEC],
        out_specs=VMEM_SPEC,
        compiler_params=pltpu.CompilerParams(vmem_limit_bytes=2 << 20),
    )(*pieces, before)


def norm_kernel(kvh_devices, p0, p1, p2, p3, residual, gain, ids, before, own, normed):
    total = residual[...].astype(jnp.float32)
    for piece in (p0, p1, p2, p3):
        total = total + piece[...].astype(jnp.float32)
    seq_count, model_dim = total.shape
    mean_square = jnp.mean(total * total, axis=-1, keepdims=True)
    rows = total * lax.rsqrt(mean_square + 1e-06) * gain[...]
    normed[:, :model_dim] = rows.astype(normed.dtype)
    lane = lax.broadcasted_iota(jnp.int32, (seq_count, normed.shape[1] - model_dim), 1)
    names = jnp.zeros(lane.shape, jnp.float32)
    for k in range(ids.shape[1]):
        names = jnp.where(ids[:, k : k + 1] == lane, 1.0, names)
    slot = [names[0:1]]
    for r in range(1, seq_count):
        slot.append(slot[-1] + names[r : r + 1])
    normed[:, model_dim:] = (names * jnp.concatenate(slot, axis=0)).astype(normed.dtype)
    place = lax.axis_index("ctx") * kvh_devices + lax.axis_index("kvh")
    width = own.shape[1]
    for p in range(model_dim // width):
        @pl.when(place == p)
        def _():
            own[...] = total[:, p * width : (p + 1) * width]


def norm(pieces, residual, gain, ids, before, kvh_devices):
    seq_count, model_dim = residual.shape
    return pl.pallas_call(
        functools.partial(norm_kernel, kvh_devices),
        out_shape=(
            pltpu.VMEM((seq_count, 256), jnp.float32),
            pltpu.VMEM((seq_count, model_dim + 128), jnp.bfloat16),
        ),
        in_specs=[VMEM_SPEC] * 7 + [ANY_SPEC],
        out_specs=(VMEM_SPEC,) * 2,
        compiler_params=pltpu.CompilerParams(vmem_limit_bytes=2 << 20),
    )(*pieces, residual, gain.reshape(1, -1), ids, before)


def weights_kernel(sizes, ids, gates, after, mix):
    kvh_devices, exp_devices, slots = sizes
    seq_count = ids.shape[0]
    shape = (seq_count, mix.shape[1])
    column = lax.broadcasted_iota(jnp.int32, shape, 1)
    device = column // (2 * slots)
    expert = device // (kvh_devices * exp_devices) * exp_devices + device % exp_devices
    weight = jnp.zeros(shape, jnp.float32)
    named = jnp.zeros(shape, jnp.float32)
    for k in range(ids.shape[1]):
        match = ids[:, k : k + 1] == expert
        weight = jnp.where(match, gates[:, k : k + 1], weight)
        named = jnp.where(match, 1.0, named)
    rank = [jnp.zeros((1, shape[1]), jnp.float32)]
    for r in range(seq_count - 1):
        rank.append(rank[-1] + named[r : r + 1])
    rank = jnp.concatenate(rank, axis=0)
    slot = (column % slots).astype(jnp.float32)
    weight = jnp.where(jnp.abs(rank - slot) < 0.5, weight, 0.0)
    half = column // slots % 2
    weight = jnp.concatenate([jnp.where(half == h, weight, 0.0) for h in range(2)], axis=0)
    high = weight.astype(jnp.bfloat16)
    mix[0 : 2 * seq_count] = high
    mix[2 * seq_count : 4 * seq_count] = (weight - high.astype(jnp.float32)).astype(jnp.bfloat16)


def mixing_weights(ids, gates, after, sizes, devices):
    slots = sizes[2]
    return pl.pallas_call(
        functools.partial(weights_kernel, sizes),
        out_shape=pltpu.VMEM((4 * ids.shape[0], devices * 2 * slots), jnp.bfloat16),
        in_specs=[VMEM_SPEC] * 2 + [ANY_SPEC],
        out_specs=VMEM_SPEC,
        compiler_params=pltpu.CompilerParams(vmem_limit_bytes=2 << 20),
    )(ids, gates, after)


def stack_kernel(p0, p1, p2, p3, before, out):
    out[...] = jnp.concatenate([p0[...], p1[...], p2[...], p3[...]], axis=0)


def stack(pieces, before):
    rows, columns = pieces[0].shape
    return pl.pallas_call(
        stack_kernel,
        out_shape=pltpu.VMEM((4 * rows, columns), pieces[0].dtype),
        in_specs=[VMEM_SPEC] * 4 + [ANY_SPEC],
        out_specs=VMEM_SPEC,
        compiler_params=pltpu.CompilerParams(vmem_limit_bytes=2 << 20),
    )(*pieces, before)


def mix_kernel(returned, mix, own, out):
    seq_count = own.shape[0]
    sums = jnp.dot(mix[...], returned[...], preferred_element_type=jnp.float32)
    sums = sums[0 : 2 * seq_count] + sums[2 * seq_count : 4 * seq_count]
    width = sums.shape[1]
    out[:, 0:width] = (own[:, 0:width] + sums[0:seq_count]).astype(out.dtype)
    out[:, width : 2 * width] = (own[:, width : 2 * width] + sums[seq_count:]).astype(out.dtype)


def mix_results(returned, mix, own):
    return pl.pallas_call(
        mix_kernel,
        out_shape=jax.ShapeDtypeStruct(own.shape, jnp.bfloat16),
        in_specs=[VMEM_SPEC] * 3,
        out_specs=VMEM_SPEC,
        compiler_params=pltpu.CompilerParams(vmem_limit_bytes=2 << 20),
    )(returned.reshape(-1, returned.shape[2]), mix, own)


def swapped(value, axes, count, mask):
    return lax.ppermute(value, axes, [(i, i ^ mask) for i in range(count)])


def body(
    queries,
    key_cache,
    value_cache,
    centroid_keys,
    centroid_values,
    selected,
    new_key,
    new_value,
    out_weight,
    residual,
    norm_gain,
    expert_ids,
    gate_weights,
    w_gate_up,
    w_down,
):
    ctx_devices = lax.axis_size("ctx")
    kvh_devices = lax.axis_size("kvh")
    exp_devices = lax.axis_size("exp")
    plane = ctx_devices * kvh_devices

    parts, out_weight = attention(
        queries,
        key_cache,
        value_cache,
        centroid_keys,
        centroid_values,
        selected,
        new_key,
        new_value,
        out_weight.reshape(-1, out_weight.shape[3]),
    )
    parts = lax.all_to_all(parts, "ctx", split_axis=0, concat_axis=0, tiled=True)

    projected = project(parts, out_weight)

    axes = ("ctx", "kvh")
    along_x = [projected] + [swapped(projected, axes, plane, m) for m in (3, 2, 1)]
    tiles = [fetch(w_gate_up, 0, 2, projected)]
    sums = sum_pieces(along_x, tiles[-1])
    along_z = [sums] + [swapped(sums, axes, plane, m) for m in (12, 4, 8)]
    tiles.append(fetch(w_gate_up, 2, 2, sums))
    own, normed = norm(along_z, residual, norm_gain, expert_ids, tiles[-1], kvh_devices)

    steps = (0, 6, 2, 4)
    along_y = [normed] + [swapped(normed, "exp", exp_devices, m) for m in steps[1:]]
    tiles.append(fetch(w_gate_up, 4, 2, normed))
    mine = stack(along_y, tiles[-1])
    other = swapped(mine, "exp", exp_devices, 1)
    order = steps + tuple(m + 1 for m in steps)
    results = experts((mine, other), tiles, w_down, order, ROW_SLOTS)
    returned = lax.all_to_all(
        results, ("ctx", "kvh", "exp"), split_axis=0, concat_axis=0, tiled=True
    )
    sizes = (kvh_devices, exp_devices, ROW_SLOTS)
    mix = mixing_weights(expert_ids, gate_weights, results, sizes, plane * exp_devices)
    return mix_results(returned, mix, own)


def solution(mesh):
    in_specs = (
        P("exp", "kvh", None, None),
        P("exp", "ctx", "kvh", None),
        P("exp", "ctx", "kvh", None),
        P("exp", "ctx", "kvh", None),
        P("exp", "ctx", "kvh", None),
        P("exp", "kvh", "ctx"),
        P("exp", "kvh", None),
        P("exp", "kvh", None),
        P("kvh", "ctx", None, None),
        P("exp", None),
        P(),
        P("exp", None),
        P("exp", None),
        P(("ctx", "exp"), None, None, "kvh"),
        P(("ctx", "exp"), "kvh", None),
    )
    out_specs = P("exp", ("ctx", "kvh"))
    return jax.shard_map(body, mesh=mesh, in_specs=in_specs, out_specs=out_specs, check_vma=False)
```
